256 devices in a mesh: gz: 4 (over y), gx: 8 (over z), gy: 8 (over x, core).
Axes of the slice: x: 4, y: 4, z: 8, core: 2. Of those that a mesh axis runs over, the one named last changes fastest.
Arguments:
- phases: float32 [4, 32, 128, 1024], P(None, 'gz', 'gx', 'gy'), may hold values from 0 to 1, as said below
- solutes: float32 [3, 32, 128, 1024], P(None, 'gz', 'gx', 'gy'), may hold values from 0 to 1
- melt: float32 [3], replicated, may hold values from 0.2 to 0.6
- shift_rows: int32 [1], replicated, may hold values from 1 to 8
- flags: int32 [4, 8, 8, 32], P('gz', 'gx', 'gy'), may hold values 0 or 1
- balance: int32 [4, 8, 8, 32], P('gz', 'gx', 'gy'), may hold values from 0 to 63, as said below
- stiffness: float32 [4, 3], replicated, may hold values from 0.04 to 0.16
- barrier: float32 [4], replicated, may hold values from 0.5 to 2
- coupling: float32 [4, 3], replicated, may hold values from -2.4 to 2.4
- slope: float32 [4], replicated, may hold values from -1 to 1
- diffusivity: float32 [4, 3], replicated, may hold values from 0.02 to 0.12
- release: float32 [4, 3], replicated, may hold values from -2 to 2
Outputs:
- phases_out: float32 [4, 32, 128, 1024], P(None, 'gz', 'gx', 'gy')
- solutes_out: float32 [3, 32, 128, 1024], P(None, 'gz', 'gx', 'gy')
- moved: float32 [8192, 7, 512], P(('gz', 'gx', 'gy'))
The draws below stay inside these ranges and needn't reach their ends.
Inputs may be any that keep to these rules, and one draw needn't show every extreme that they name: `phases`: each cell's 4 fractions are nonnegative and sum to one. `balance`: within a growth slab, a device block gives exactly 2 tiles to each owner that it gives any, and every owner receives exactly 32 tiles.
All inputs are finite; a program needn't handle non-finite values. No bound on the sum of `flags` on one device may be relied on, other than what follows from the above.
Results may differ from the reference program's by a relative error of at most 0.0001.
Values sent between devices are 32-bit elements; how exact they have to be, the bound alone decides.
No kernel may reach another device: no remote copies, remote signals or barrier semaphores. Data moves between devices by JAX's collectives and lax.ppermute only.
A program may use at most 64 MiB of HBM per device.

```python
import math
import jax
import jax.numpy as jnp
from jax import lax

PHASES = 4
SOLUTES = 3
CZ = 8
CX = 16
CY = 128
TS = 8
STEPS = 2
NZ = 32
NX = 128
NY = 1024
TPD = 32
MOST = 2
MOVED = 8192
N_GZ = 4
N_GX = 8
N_GY = 8


def draw_phases(key, part):
    key = jax.random.fold_in(key, 11)
    shape = (PHASES, NZ, NX, NY)
    weights = jax.random.uniform(key, shape, dtype=jnp.float32, minval=0.05, maxval=1.0)
    return weights / jnp.sum(weights, axis=0, keepdims=True)


def draw_balance(key, part):
    key = jax.random.fold_in(key, 7)
    owners = N_GX * N_GY

    def slab_table(slab_key):
        peer_key, order_key = jax.random.split(slab_key)
        shuffled = jax.random.permutation(peer_key, owners)
        peers = (shuffled + (owners // 2 - shuffled[0])) % owners
        order = jax.random.permutation(order_key, TPD)
        offset = peers[order // MOST]
        source = jnp.arange(owners)[:, None]
        return ((source + offset[None, :]) % owners).astype(jnp.int32)
    table = jax.vmap(slab_table)(jax.random.split(key, N_GZ))
    return table.reshape(N_GZ, N_GX, N_GY, TPD)


def touch_ends(values, rng, low, high):
    dims = values.shape
    spot = [jax.random.randint(jax.random.fold_in(rng, axis), (), 0, dims[axis]) for axis in range(len(dims))]
    values = values.at[tuple(spot)].set(low)
    longest = dims.index(max(dims))
    spot[longest] = (spot[longest] + 1) % dims[longest]
    return values.at[tuple(spot)].set(high)


def levels(stream_key, shape, pieces, smallest, high):
    level, own = 1.0, jax.random.fold_in(stream_key, 6)
    for position, blocks in pieces:
        heights = jnp.exp(jax.random.uniform(jax.random.fold_in(own, position), (blocks,), jnp.float32, smallest / len(pieces), high / len(pieces)))
        level = level * jnp.repeat(heights, shape[position] // blocks).reshape([-1 if axis == position else 1 for axis in range(len(shape))])
    return level


def normal_values(stream_key, shape, width, limit, kind=jnp.bfloat16):
    entries = width * jax.random.normal(stream_key, shape, jnp.float32)
    return jnp.clip(entries, min=-limit, max=limit).astype(kind)


def setup_inputs(seed: int = 0) -> dict:
    splits = jax.random.split(jax.random.key(seed), 13)
    phases = draw_phases(jax.random.fold_in(splits[12], 71), 0)
    solutes = jnp.clip(1.0 * jax.random.uniform(splits[1], (SOLUTES, NZ, NX, NY), jnp.float32) ** levels(splits[1], (SOLUTES, NZ, NX, NY), ((1, 4), (2, 8), (3, 8)), -0.2, 0.2), 0.0, 1.0)
    melt = jnp.clip(jax.random.uniform(splits[2], (SOLUTES,), jnp.float32, 0.2, 0.6), 0.2, 0.6)
    shift_rows = jax.random.randint(splits[3], (1,), 1, CZ + 1).astype(jnp.int32)
    flags = touch_ends((jax.random.randint(splits[4], (N_GZ, N_GX, N_GY, TPD), 0, 2) < 1).astype(jnp.int32), jax.random.fold_in(splits[4], 1), 0, 1)
    balance = draw_balance(jax.random.fold_in(splits[12], 71), 0)
    stiffness = jnp.clip(jnp.exp(jax.random.uniform(splits[6], (PHASES, 3), jnp.float32, math.log(0.04), math.log(0.16))), 0.04, 0.16)
    barrier = jnp.clip(jnp.exp(jax.random.uniform(splits[7], (PHASES,), jnp.float32, math.log(0.5), math.log(2.0))), 0.5, 2.0)
    coupling = normal_values(splits[8], (PHASES, SOLUTES), 0.6, 2.4, jnp.float32)
    slope = jnp.clip(jax.random.uniform(splits[9], (PHASES,), jnp.float32, -1.0, 1.0), -1.0, 1.0)
    diffusivity = jnp.clip(jnp.exp(jax.random.uniform(splits[10], (PHASES, SOLUTES), jnp.float32, math.log(0.02), math.log(0.12))), 0.02, 0.12)
    release = normal_values(splits[11], (PHASES, SOLUTES), 0.5, 2.0, jnp.float32)
    return dict(phases=phases, solutes=solutes, melt=melt, shift_rows=shift_rows, flags=flags, balance=balance, stiffness=stiffness, barrier=barrier, coupling=coupling, slope=slope, diffusivity=diffusivity, release=release)


def column_of(values):
    return values[:, None, None, None]


def melt_column(melt):
    return jnp.concatenate([jnp.array([0.0, 0.0, 0.0, 1.0], dtype=melt.dtype), melt])


def density(fractions, diffusivity):
    summed = column_of(diffusivity[0]) * fractions[0]
    for phase_num in range(1, 4):
        summed = summed + column_of(diffusivity[phase_num]) * fractions[phase_num]
    return summed


def advance(fields, neighbours, flag_cells, height, stiffness, barrier, coupling, slope, diffusivity, release):
    fractions = fields[:4]
    solute_part = fields[4:]
    laplace = jnp.zeros_like(fractions)
    for axis_num in range(3):
        upper_side, lower_side = neighbours[axis_num]
        laplace = laplace + column_of(stiffness[:, axis_num]) * (upper_side[:4] + lower_side[:4] - 2.0 * fractions)
    interface = fractions * (1.0 - fractions)
    driving = column_of(slope) * height
    for solute_num in range(3):
        driving = driving + column_of(coupling[:, solute_num]) * solute_part[solute_num]
    growth_rate = flag_cells * (laplace + column_of(barrier) * interface * (2.0 * fractions - 1.0) + interface * driving)
    change = growth_rate - 0.25 * jnp.sum(growth_rate, axis=0)
    own_density = density(fractions, diffusivity)
    transport = jnp.zeros_like(solute_part)
    for upper_side, lower_side in neighbours:
        for beside in (upper_side, lower_side):
            transport = transport + 0.5 * (own_density + density(beside[:4], diffusivity)) * (beside[4:] - solute_part)
    released = column_of(release[0]) * change[0]
    for phase_num in range(1, 4):
        released = released + column_of(release[phase_num]) * change[phase_num]
    return jnp.concatenate([fractions + change, solute_part + transport + released], axis=0)


def neighbours_of(fields):
    z_upper = jnp.concatenate([fields[:, 1:], fields[:, -1:]], axis=1)
    z_lower = jnp.concatenate([fields[:, :1], fields[:, :-1]], axis=1)
    x_upper = jnp.roll(fields, -1, axis=2)
    x_lower = jnp.roll(fields, 1, axis=2)
    y_upper = jnp.roll(fields, -1, axis=3)
    y_lower = jnp.roll(fields, 1, axis=3)
    return [(z_upper, z_lower), (x_upper, x_lower), (y_upper, y_lower)]


def reference(phases, solutes, melt, shift_rows, flags, balance, stiffness, barrier, coupling, slope, diffusivity, release):
    components = PHASES + SOLUTES
    fields = jnp.concatenate([phases, solutes], axis=0)
    incoming = jnp.broadcast_to(column_of(melt_column(melt)), (components, CZ, NX, NY))
    extended = jnp.concatenate([fields, incoming], axis=1)
    fields = lax.dynamic_slice_in_dim(extended, shift_rows[0].astype(jnp.int32), NZ, 1)
    tiles_z = CZ // TS
    tiles_x = CX // TS
    tiles_y = CY // TS
    flag_grid = flags.reshape(N_GZ, N_GX, N_GY, tiles_z, tiles_x, tiles_y).transpose(0, 3, 1, 4, 2, 5)
    flag_grid = flag_grid.reshape(NZ // TS, NX // TS, NY // TS)
    flag_cells = jnp.repeat(jnp.repeat(jnp.repeat(flag_grid, TS, 0), TS, 1), TS, 2).astype(fields.dtype)
    height = ((jnp.arange(NZ).astype(fields.dtype) + 0.5) / NZ - 0.5).reshape(1, NZ, 1, 1)
    for step_num in range(STEPS):
        fields = advance(fields, neighbours_of(fields), flag_cells, height, stiffness, barrier, coupling, slope, diffusivity, release)
    owners = N_GX * N_GY
    tiles = fields.reshape(components, N_GZ, tiles_z, TS, N_GX, tiles_x, TS, N_GY, tiles_y, TS)
    tiles = tiles.transpose(1, 4, 7, 2, 5, 8, 0, 3, 6, 9).reshape(N_GZ, owners * TPD, components, TS ** 3)
    serial = jnp.arange(owners * TPD).astype(jnp.int32)
    sort_keys = balance.reshape(N_GZ, owners * TPD).astype(jnp.int32) * (owners * TPD) + serial[None, :]
    order = jnp.argsort(sort_keys, axis=1)
    moved = jnp.take_along_axis(tiles, order[:, :, None, None], axis=1).reshape(MOVED, components, TS ** 3)
    return fields[:4], fields[4:], moved
```

```python
import jax
import jax.numpy as jnp
from jax import lax
from jax.experimental import pallas as pl
from jax.experimental.pallas import tpu as pltpu
from jax.sharding import PartitionSpec as P

CZ, CX, CY = 8, 16, 128
KEPT = 6
WINDOW = CZ + 4
ROWS = CZ * CX
X_ROWS = 18
MARKER = 3.0e38
LIMIT = 1.0e30
F32 = jnp.float32

VMEM = pl.BlockSpec(memory_space=pltpu.VMEM)
SMEM = pl.BlockSpec(memory_space=pltpu.SMEM)


def lanes_of(rows):
    return lax.broadcasted_iota(jnp.int32, (rows, 128), 1)


def sublanes_of(rows):
    return lax.broadcasted_iota(jnp.int32, (rows, 128), 0)


def flag_row(flags_ref, b):
    group = lanes_of(8) // 8
    row = jnp.zeros((8, 128), F32)
    for d in range(16):
        row = jnp.where(group == d, flags_ref[0, 0, 0, b * 16 + d].astype(F32), row)
    return row


def kept(phases_ref, solutes_ref, c, z):
    return phases_ref[c, z] if c < 3 else solutes_ref[c - 3, z]


def pack_z(phases_ref, solutes_ref, flags_ref, down_ref, down2_ref, up_ref):
    flags = [flag_row(flags_ref, b) for b in range(2)]
    for c in range(KEPT):
        for z in range(CZ):
            plane = kept(phases_ref, solutes_ref, c, z)
            down_ref[c * CZ + z] = plane
            if z < 2:
                down2_ref[c * 2 + z] = plane
            if z == CZ - 1:
                up_ref[c] = plane
    for b in range(2):
        down_ref[KEPT * CZ, b * 8 : b * 8 + 8] = flags[b]
        up_ref[KEPT, b * 8 : b * 8 + 8] = flags[b]


def frame(
    phases_ref, solutes_ref, above_ref, above2_ref, below_ref, flags_ref, melt_ref, shift_ref, slab_ref,
    window_ref, low_ref, high_ref, raw_ref,
):
    slab = slab_ref[0]
    shift = shift_ref[0]
    at_bottom = slab == 0
    at_top = slab == 3
    for c in range(KEPT):
        fresh = jnp.full((CX, 128), 0.0 if c < 3 else melt_ref[c - 3], F32)
        raw_ref[c, 0:CX] = below_ref[c]
        for z in range(CZ):
            raw_ref[c, (1 + z) * CX : (2 + z) * CX] = kept(phases_ref, solutes_ref, c, z)
            raw_ref[c, (9 + z) * CX : (10 + z) * CX] = jnp.where(at_top, fresh, above_ref[c * CZ + z])
        for z in range(2):
            raw_ref[c, (17 + z) * CX : (18 + z) * CX] = jnp.where(slab >= 2, fresh, above2_ref[c * 2 + z])
        for w in range(WINDOW):
            start = pl.multiple_of((shift - 1 + w) * CX, CX)
            window_ref[c, w * CX : (w + 1) * CX] = raw_ref[c, pl.ds(start, CX)]

        @pl.when(at_bottom)
        def _(c=c):
            window_ref[c, CX : 2 * CX] = window_ref[c, 2 * CX : 3 * CX]

        @pl.when(at_top)
        def _(c=c):
            window_ref[c, 10 * CX : 11 * CX] = window_ref[c, 9 * CX : 10 * CX]

        for ref, near, far in ((low_ref, 0, 1), (high_ref, 15, 14)):
            ref[c * X_ROWS : c * X_ROWS + 8] = window_ref[c, pl.ds(CX + near, 8, stride=CX)]
            ref[c * X_ROWS + 8 : c * X_ROWS + 10] = window_ref[c, pl.ds(9 * CX + near, 2, stride=CX)]
            ref[c * X_ROWS + 10 : c * X_ROWS + 18] = window_ref[c, pl.ds(2 * CX + far, 8, stride=CX)]
    low_ref[KEPT * X_ROWS : KEPT * X_ROWS + 4] = flag_row(flags_ref, 0)[:4]
    high_ref[KEPT * X_ROWS : KEPT * X_ROWS + 4] = flag_row(flags_ref, 1)[:4]


def pack_y(window_ref, before_ref, after_ref, flags_ref, out_ref, inner_ref, ends_ref, sides_ref):
    def gather(rows, value_of):
        lane = lanes_of(rows)
        packed = jnp.zeros((rows, 128), F32)
        for c in range(KEPT):
            moved = pltpu.roll(value_of(c), 2 + 4 * c, 1)
            packed = jnp.where((lane >= 4 * c) & (lane < 4 * c + 4), moved, packed)
        return packed

    flags = jnp.concatenate([flag_row(flags_ref, b) for b in range(2)], axis=0)
    flags = pltpu.roll(flags, 25, 1)
    flag_lane = (lanes_of(CX) == 24) | (lanes_of(CX) == 25)
    for z in range(CZ):
        packed = gather(CX, lambda c: window_ref[c, (z + 2) * CX : (z + 3) * CX])
        inner_ref[z * CX : (z + 1) * CX] = jnp.where(flag_lane, flags, packed)
    ends_ref[...] = jnp.zeros((128, 128), F32)
    ends_ref[0:CX] = gather(CX, lambda c: window_ref[c, CX : 2 * CX])
    ends_ref[112:128] = gather(CX, lambda c: window_ref[c, 10 * CX : 11 * CX])
    sides_ref[...] = jnp.zeros((128, 128), F32)
    sides_ref[pl.ds(0, 8, stride=CX)] = gather(8, lambda c: before_ref[c * X_ROWS + 1 : c * X_ROWS + 9])
    sides_ref[pl.ds(15, 8, stride=CX)] = gather(8, lambda c: after_ref[c * X_ROWS + 1 : c * X_ROWS + 9])
    out_ref[0:32] = inner_ref[...].T[0:32]
    out_ref[32:56] = ends_ref[...].T[0:24]
    out_ref[56:80] = sides_ref[...].T[0:24]


def read_parameters(stiffness_ref, barrier_ref, coupling_ref, slope_ref, diffusivity_ref, release_ref):
    return dict(
        stiffness=[[stiffness_ref[a, e] for e in range(3)] for a in range(4)],
        barrier=[barrier_ref[a] for a in range(4)],
        coupling=[[coupling_ref[a, k] for k in range(3)] for a in range(4)],
        slope=[slope_ref[a] for a in range(4)],
        base=[0.5 * diffusivity_ref[3, k] for k in range(3)],
        excess=[[0.5 * (diffusivity_ref[a, k] - diffusivity_ref[3, k]) for k in range(3)] for a in range(3)],
        release=[[release_ref[a, k] for k in range(3)] for a in range(4)],
    )


def advance(own, neighbours, flag, height, par):
    fractions = list(own[:3])
    fractions.append(1.0 - (own[0] + own[1] + own[2]))
    solutes = own[3:]

    def half_density(at, k):
        return par["base"][k] + (
            par["excess"][0][k] * at[0] + par["excess"][1][k] * at[1] + par["excess"][2][k] * at[2]
        )

    own_density = [half_density(own, k) for k in range(3)]
    gains = [None] * 3
    laplace = [None] * 4
    for e, (upper, lower) in enumerate(neighbours):
        curve = [upper[a] + lower[a] - 2.0 * own[a] for a in range(3)]
        curve.append(-(curve[0] + curve[1] + curve[2]))
        for a in range(4):
            term = par["stiffness"][a][e] * curve[a]
            laplace[a] = term if laplace[a] is None else laplace[a] + term
        for beside in (upper, lower):
            for k in range(3):
                flow = (own_density[k] + half_density(beside, k)) * (beside[3 + k] - solutes[k])
                gains[k] = flow if gains[k] is None else gains[k] + flow
    rates = []
    for a in range(4):
        p = fractions[a]
        drive = par["slope"][a] * height + par["barrier"][a] * (2.0 * p - 1.0)
        for k in range(3):
            drive = drive + par["coupling"][a][k] * solutes[k]
        rates.append(flag * (laplace[a] + p * (1.0 - p) * drive))
    mean = 0.25 * (rates[0] + rates[1] + rates[2] + rates[3])
    changes = [rate - mean for rate in rates]
    after = [fractions[a] + changes[a] for a in range(4)]
    for k in range(3):
        released = par["release"][0][k] * changes[0]
        for a in range(1, 4):
            released = released + par["release"][a][k] * changes[a]
        after.append(solutes[k] + gains[k] + released)
    return after[:3] + after[4:], after[3]


def steps(
    window_ref, before_ref, after_ref, own_y_ref, left_ref, right_ref, above_ref, below_ref,
    flags_ref, slots_ref, slab_ref,
    stiffness_ref, barrier_ref, coupling_ref, slope_ref, diffusivity_ref, release_ref,
    phases_ref, solutes_ref, send_ref,
    edge_ref, turned_ref, first_ref, xface_ref, final_ref,
):
    slab = slab_ref[0]
    at_bottom = slab == 0
    at_top = slab == 3
    par = read_parameters(stiffness_ref, barrier_ref, coupling_ref, slope_ref, diffusivity_ref, release_ref)
    first_row = (slab * CZ).astype(F32)

    def height_of(z):
        return (first_row + z + 0.5) / 32.0 - 0.5

    lane16, lane8, sub16 = lanes_of(CX), lanes_of(8), sublanes_of(CX)
    flags = jnp.concatenate([flag_row(flags_ref, b) for b in range(2)], axis=0)

    edge_ref[...] = jnp.zeros((128, 128), F32)
    for group, start in ((0, 0), (1, 32), (2, 56)):
        for c in range(KEPT):
            at = group * 12 + 2 * c
            edge_ref[at : at + 1] = right_ref[start + 4 * c + 2 : start + 4 * c + 3]
            edge_ref[at + 1 : at + 2] = left_ref[start + 4 * c + 1 : start + 4 * c + 2]
    turned_ref[...] = edge_ref[...].T

    def beside_y(value, rows, column):
        lane = lane16 if value.shape[0] == CX else lane8
        fill = pltpu.roll(rows, 127 - column, 1)
        upper = jnp.where(lane == 127, fill, pltpu.roll(value, 127, 1))
        lower = jnp.where(lane == 0, fill, pltpu.roll(value, 1, 1))
        return upper, lower

    def beside_x(ref, c, start, low_row, high_row):
        upper = jnp.where(sub16 == 15, high_row, ref[c, start + 1 : start + 1 + CX])
        lower = jnp.where(sub16 == 0, low_row, ref[c, start - 1 : start - 1 + CX])
        return upper, lower

    def split(pairs):
        return ([pair[0] for pair in pairs], [pair[1] for pair in pairs])

    for w in range(1, WINDOW - 1):
        z = w - 2
        start = w * CX
        own = [window_ref[c, start : start + CX] for c in range(KEPT)]
        along_z = (
            [window_ref[c, start + CX : start + 2 * CX] for c in range(KEPT)],
            [window_ref[c, start - CX : start] for c in range(KEPT)],
        )
        along_x = split(
            [
                beside_x(
                    window_ref, c, start,
                    before_ref[c * X_ROWS + z + 1 : c * X_ROWS + z + 2],
                    after_ref[c * X_ROWS + z + 1 : c * X_ROWS + z + 2],
                )
                for c in range(KEPT)
            ]
        )
        if z == -1:
            rows, group, flag = turned_ref[0:CX], 1, below_ref[KEPT]
        elif z == CZ:
            rows, group, flag = turned_ref[112:128], 1, above_ref[KEPT * CZ]
        else:
            rows, group, flag = turned_ref[z * CX : (z + 1) * CX], 0, flags
        along_y = split([beside_y(own[c], rows, group * 12 + 2 * c) for c in range(KEPT)])
        result, _ = advance(own, (along_z, along_x, along_y), flag, height_of(z), par)
        for c in range(KEPT):
            first_ref[c, (w - 1) * CX : w * CX] = result[c]

    @pl.when(at_bottom)
    def _():
        for c in range(KEPT):
            first_ref[c, 0:CX] = first_ref[c, CX : 2 * CX]

    @pl.when(at_top)
    def _():
        for c in range(KEPT):
            first_ref[c, 9 * CX : 10 * CX] = first_ref[c, 8 * CX : 9 * CX]

    face_height = height_of(sublanes_of(8).astype(F32))
    for side, ref, x in ((0, before_ref, 0), (1, after_ref, 15)):
        own = [ref[c * X_ROWS + 1 : c * X_ROWS + 9] for c in range(KEPT)]
        along_z = (
            [ref[c * X_ROWS + 2 : c * X_ROWS + 10] for c in range(KEPT)],
            [ref[c * X_ROWS : c * X_ROWS + 8] for c in range(KEPT)],
        )
        along_x = (
            [ref[c * X_ROWS + 10 : c * X_ROWS + 18] for c in range(KEPT)],
            [window_ref[c, pl.ds(2 * CX + x, 8, stride=CX)] for c in range(KEPT)],
        )
        rows = turned_ref[pl.ds(x, 8, stride=CX)]
        along_y = split([beside_y(own[c], rows, 24 + 2 * c) for c in range(KEPT)])
        flag = ref[KEPT * X_ROWS : KEPT * X_ROWS + 1]
        result, _ = advance(own, (along_z, along_x, along_y), flag, face_height, par)
        for c in range(KEPT):
            xface_ref[side * KEPT + c] = result[c]

    sub8 = sublanes_of(8)

    def both(right_row, left_row):
        return jnp.where(sub8 == 0, right_row, left_row)

    def lifted(c, start):
        return both(
            right_ref[start + 4 * c + 2 : start + 4 * c + 3],
            left_ref[start + 4 * c + 1 : start + 4 * c + 2],
        )

    own = [lifted(c, 0) for c in range(KEPT)]
    ends = [lifted(c, 32) for c in range(KEPT)]
    sides = [lifted(c, 56) for c in range(KEPT)]
    outer = [both(right_ref[4 * c + 3 : 4 * c + 4], left_ref[4 * c : 4 * c + 1]) for c in range(KEPT)]
    inner = [both(own_y_ref[4 * c + 1 : 4 * c + 2], own_y_ref[4 * c + 2 : 4 * c + 3]) for c in range(KEPT)]
    along_z = (
        [jnp.where(lane8 >= 112, ends[c], pltpu.roll(own[c], 112, 1)) for c in range(KEPT)],
        [jnp.where(lane8 < 16, ends[c], pltpu.roll(own[c], 16, 1)) for c in range(KEPT)],
    )
    along_x = (
        [jnp.where(lane8 % 16 == 15, sides[c], pltpu.roll(own[c], 127, 1)) for c in range(KEPT)],
        [jnp.where(lane8 % 16 == 0, sides[c], pltpu.roll(own[c], 1, 1)) for c in range(KEPT)],
    )
    flag = both(right_ref[25:26], left_ref[24:25])
    result, _ = advance(
        own, (along_z, along_x, (outer, inner)), flag, height_of((lane8 // 16).astype(F32)), par
    )
    for c in range(KEPT):
        edge_ref[2 * c : 2 * c + 2] = result[c][0:2]
    turned_ref[...] = edge_ref[...].T

    for z in range(CZ):
        start = (z + 1) * CX
        own = [first_ref[c, start : start + CX] for c in range(KEPT)]
        along_z = (
            [first_ref[c, start + CX : start + 2 * CX] for c in range(KEPT)],
            [first_ref[c, start - CX : start] for c in range(KEPT)],
        )
        along_x = split(
            [
                beside_x(first_ref, c, start, xface_ref[c, z : z + 1], xface_ref[KEPT + c, z : z + 1])
                for c in range(KEPT)
            ]
        )
        rows = turned_ref[z * CX : (z + 1) * CX]
        along_y = split([beside_y(own[c], rows, 2 * c) for c in range(KEPT)])
        result, last = advance(own, (along_z, along_x, along_y), flags, height_of(z), par)
        for c in range(3):
            phases_ref[c, z] = result[c]
            solutes_ref[c, z] = result[3 + c]
        phases_ref[3, z] = last
        for c in range(KEPT):
            final_ref[c * ROWS + z * CX : c * ROWS + (z + 1) * CX] = result[c]

    for owner in range(64):
        send_ref[2 * owner, 0:1] = jnp.full((1, 128), MARKER, F32)
    group = lane8 // 8
    for b in range(2):
        for q in range(4):
            parts = []
            for i in range(16):
                row = (2 * q + i // 8) * CX + b * 8 + i % 8
                parts.append(final_ref[pl.ds(row, 8, stride=ROWS)])
            for step in (8, 4, 2, 1):
                keep = (group & step) == 0
                swapped = list(parts)
                for i in range(16):
                    if i & step == 0:
                        one, two = parts[i], parts[i + step]
                        swapped[i] = jnp.where(keep, one, pltpu.roll(two, step * 8, 1))
                        swapped[i + step] = jnp.where(keep, pltpu.roll(one, 128 - step * 8, 1), two)
                parts = swapped
            for d in range(16):
                send_ref[slots_ref[b * 16 + d], 6 * q : 6 * q + 6] = parts[d][0:6]


def place(arrived_ref, moved_ref):
    sub16 = sublanes_of(16)
    weight = jnp.zeros((16, 128), F32)
    for i in range(16):
        weight = jnp.where((sub16 == i) & (lanes_of(16) == 0), float(2**i), weight)
    masks = []
    for block in range(4):
        first = jnp.concatenate([arrived_ref[2 * (block * 16 + i), 0:1] for i in range(16)], axis=0)
        masks.append(jnp.sum(jnp.where(first < LIMIT, weight, 0.0)).astype(jnp.int32))
    count = jnp.int32(0)
    for block in range(4):

        def one_source(i, count, block=block):
            present = (masks[block] >> i) & 1
            source = block * 16 + i

            @pl.when((present == 1) & (count < 31))
            def _():
                for e in range(2):
                    for q in range(4):
                        part = arrived_ref[2 * source + e, 6 * q : 6 * q + 6]
                        span = slice(q * 128, (q + 1) * 128)
                        moved_ref[count + e, 0:3, span] = part[0:3]
                        moved_ref[count + e, 3:4, span] = 1.0 - (part[0:1] + part[1:2] + part[2:3])
                        moved_ref[count + e, 4:7, span] = part[3:6]

            return count + 2 * present

        count = lax.fori_loop(0, 16, one_source, count)


def shape_of(*dims):
    return jax.ShapeDtypeStruct(dims, F32)


PARAMS = pltpu.CompilerParams(vmem_limit_bytes=32 * 1024 * 1024)


def call(body, ins, outs, scratch=(), flops=0):
    return pl.pallas_call(
        body,
        in_specs=list(ins),
        out_specs=[VMEM] * len(outs),
        out_shape=list(outs),
        scratch_shapes=list(scratch),
        compiler_params=PARAMS,
        cost_estimate=pl.CostEstimate(flops=flops, bytes_accessed=1000000, transcendentals=0),
    )


def shifted(value, axis, by, wrap):
    count = lax.axis_size(axis)
    pairs = [
        (source, (source + by) % count) for source in range(count) if wrap or 0 <= source + by < count
    ]
    return lax.ppermute(value, axis, pairs)


def per_device(
    phases, solutes, melt, shift_rows, flags, balance,
    stiffness, barrier, coupling, slope, diffusivity, release,
):
    slab = lax.axis_index("gz").astype(jnp.int32).reshape(1)
    owner_list = balance.reshape(32)
    serial = jnp.arange(32)
    earlier = jnp.sum(
        ((owner_list[:, None] == owner_list[None, :]) & (serial[None, :] < serial[:, None])).astype(jnp.int32),
        axis=1,
    )
    slots = owner_list * 2 + earlier

    down, down2, up = call(
        pack_z,
        [VMEM, VMEM, SMEM],
        [shape_of(KEPT * CZ + 1, CX, 128), shape_of(KEPT * 2, CX, 128), shape_of(KEPT + 1, CX, 128)],
    )(phases, solutes, flags)
    above = shifted(down, "gz", -1, False)
    above2 = shifted(down2, "gz", -2, False)
    below = shifted(up, "gz", 1, False)

    window, low, high = call(
        frame,
        [VMEM] * 5 + [SMEM] * 4,
        [shape_of(KEPT, WINDOW * CX, 128), shape_of(112, 128), shape_of(112, 128)],
        [pltpu.VMEM((KEPT, 19 * CX, 128), F32)],
    )(phases, solutes, above, above2, below, flags, melt, shift_rows, slab)
    before = shifted(high, "gx", 1, True)
    after = shifted(low, "gx", -1, True)

    (faces,) = call(
        pack_y,
        [VMEM] * 3 + [SMEM],
        [shape_of(80, 128)],
        [pltpu.VMEM((128, 128), F32)] * 3,
    )(window, before, after, flags)
    left = shifted(faces, "gy", 1, True)
    right = shifted(faces, "gy", -1, True)

    phases_out, solutes_out, send = call(
        steps,
        [VMEM] * 8 + [SMEM] * 9,
        [shape_of(4, CZ, CX, CY), shape_of(3, CZ, CX, CY), shape_of(128, 24, 128)],
        [
            pltpu.VMEM((128, 128), F32),
            pltpu.VMEM((128, 128), F32),
            pltpu.VMEM((KEPT, 10 * CX, 128), F32),
            pltpu.VMEM((2 * KEPT, 8, 128), F32),
            pltpu.VMEM((8 * ROWS, 128), F32),
        ],
    )(
        window, before, after, faces, left, right, above, below, flags, slots, slab,
        stiffness, barrier, coupling, slope, diffusivity, release,
    )
    arrived = lax.all_to_all(send, ("gx", "gy"), split_axis=0, concat_axis=0, tiled=True)
    (moved,) = call(place, [VMEM], [shape_of(32, 7, 512)])(arrived)
    return phases_out, solutes_out, moved


def solution(mesh):
    block = P(None, "gz", "gx", "gy")
    table = P("gz", "gx", "gy", None)
    return jax.shard_map(
        per_device,
        mesh=mesh,
        in_specs=(block, block, P(), P(), table, table, P(), P(), P(), P(), P(), P()),
        out_specs=(block, block, P(("gz", "gx", "gy"), None, None)),
        check_vma=False,
    )
```

```python
import jax
import jax.numpy as jnp
from jax import lax
from jax.experimental import pallas as pl
from jax.experimental.pallas import tpu as pltpu
from jax.sharding import PartitionSpec as P

CZ, CX, CY = 8, 16, 128
KEPT = 6
WINDOW = CZ + 4
ROWS = CZ * CX
FAR = 80
MARKER = 3.0e38
LIMIT = 1.0e30
F32 = jnp.float32

VMEM = pl.BlockSpec(memory_space=pltpu.VMEM)
SMEM = pl.BlockSpec(memory_space=pltpu.SMEM)
ANY = pl.BlockSpec(memory_space=pl.ANY)


def lanes_of(rows):
    return lax.broadcasted_iota(jnp.int32, (rows, 128), 1)


def sublanes_of(rows):
    return lax.broadcasted_iota(jnp.int32, (rows, 128), 0)


def flag_row(flags_ref, b):
    group = lanes_of(8) // 8
    row = jnp.zeros((8, 128), F32)
    for d in range(16):
        row = jnp.where(group == d, flags_ref[0, 0, 0, b * 16 + d].astype(F32), row)
    return row


LAYERS = (0, 1, 14, 15)
STRIP = 24


def gather(rows, value_of):
    lane = lanes_of(rows)
    packed = jnp.zeros((rows, 128), F32)
    for c in range(KEPT):
        moved = pltpu.roll(value_of(c), 2 + 4 * c, 1)
        packed = jnp.where((lane >= 4 * c) & (lane < 4 * c + 4), moved, packed)
    return packed


def pack_z(
    phases_ref, solutes_ref, flags_ref, shift_ref, melt_ref,
    bulk_ref, second_ref, last_ref, strip_ref, columns_ref, meta_ref,
    flags_now, shift_now, melt_now, copied, small_copied,
):
    copies = [
        pltpu.make_async_copy(flags_ref, flags_now, small_copied.at[0]),
        pltpu.make_async_copy(shift_ref, shift_now, small_copied.at[1]),
        pltpu.make_async_copy(melt_ref, melt_now, small_copied.at[2]),
    ]
    for c in range(KEPT):
        source = phases_ref.at[c] if c < 3 else solutes_ref.at[c - 3]
        copies.append(pltpu.make_async_copy(source, bulk_ref.at[pl.ds(c * ROWS, ROWS)], copied.at[c]))
    for copy in copies:
        copy.start()
    for copy in copies:
        copy.wait()

    flags = jnp.concatenate([flag_row(flags_now, b) for b in range(2)], axis=0)
    bulk_ref[KEPT * ROWS : KEPT * ROWS + CX] = flags
    last_ref[KEPT * CX : (KEPT + 1) * CX] = flags
    meta_ref[...] = jnp.zeros((8, 128), F32)
    meta_ref[0:1] = jnp.full((1, 128), shift_now[0].astype(F32), F32)
    for k in range(3):
        meta_ref[1 + k : 2 + k] = jnp.full((1, 128), melt_now[k], F32)
    for c in range(KEPT):
        second_ref[2 * c * CX : 2 * (c + 1) * CX] = bulk_ref[c * ROWS : c * ROWS + 2 * CX]
        last_ref[c * CX : (c + 1) * CX] = bulk_ref[c * ROWS + 7 * CX : (c + 1) * ROWS]
        for n, x in enumerate(LAYERS):
            strip_ref[pl.ds(n * KEPT + c, 8, stride=STRIP)] = bulk_ref[pl.ds(c * ROWS + x, 8, stride=CX)]
    flags = pltpu.roll(flags, 25, 1)
    flag_lane = (lanes_of(CX) == 24) | (lanes_of(CX) == 25)
    for z in range(CZ):
        packed = gather(CX, lambda c: bulk_ref[c * ROWS + z * CX : c * ROWS + (z + 1) * CX])
        columns_ref[z * CX : (z + 1) * CX] = jnp.where(flag_lane, flags, packed)
    strip_ref[8 * STRIP : 8 * STRIP + 32] = columns_ref[...].T[0:32]


def window_ends(meta_ref, slab_ref):
    shift = jnp.max(meta_ref[0:1]).astype(jnp.int32)
    slab = slab_ref[0]
    return shift, jnp.where(slab == 0, shift, shift - 1), jnp.where(slab == 3, shift + 7, shift + 8)


def pack_x(own_ref, above_ref, above2_ref, bulk_ref, meta_ref, slab_ref, low_ref, high_ref, raw_ref):
    slab = slab_ref[0]
    shift, first, last = window_ends(meta_ref, slab_ref)
    fresh = jnp.zeros((STRIP, 128), F32)
    sub = sublanes_of(STRIP) % KEPT
    for k in range(3):
        fresh = jnp.where(sub == 3 + k, meta_ref[1 + k : 2 + k], fresh)
    raw_ref[0 : 8 * STRIP] = own_ref[0 : 8 * STRIP]
    for z in range(CZ):
        rows = slice((8 + z) * STRIP, (9 + z) * STRIP)
        raw_ref[rows] = jnp.where(slab == 3, fresh, above_ref[z * STRIP : (z + 1) * STRIP])
    for c in range(KEPT):
        for n, x in enumerate(LAYERS):
            at = 16 * STRIP + n * KEPT + c
            raw_ref[at : at + 1] = above2_ref[2 * c * CX + x : 2 * c * CX + x + 1]

    @pl.when(slab >= 2)
    def _():
        raw_ref[16 * STRIP : 17 * STRIP] = fresh

    for i in range(10):
        row = first if i == 0 else last if i == 9 else shift + (i - 1)
        value = raw_ref[pl.ds(pl.multiple_of(row * STRIP, 8), STRIP)]
        low_ref[i * 8 : i * 8 + KEPT] = value[0:6]
        high_ref[i * 8 : i * 8 + KEPT] = value[18:24]
        if 0 < i < 9:
            low_ref[FAR + (i - 1) * 8 : FAR + (i - 1) * 8 + KEPT] = value[6:12]
            high_ref[FAR + (i - 1) * 8 : FAR + (i - 1) * 8 + KEPT] = value[12:18]
    low_ref[KEPT : KEPT + 1] = bulk_ref[KEPT * ROWS : KEPT * ROWS + 1]
    high_ref[KEPT : KEPT + 1] = bulk_ref[KEPT * ROWS + 15 : KEPT * ROWS + 16]


def turn_columns(columns_ref, above_ref, above2_ref, meta_ref, slab_ref, out_ref, raw_ref, wide_ref):
    slab = slab_ref[0]
    shift, first, last = window_ends(meta_ref, slab_ref)
    fresh = jnp.zeros((CX, 128), F32)
    part = lanes_of(CX) // 4
    for k in range(3):
        fresh = jnp.where(part == 3 + k, meta_ref[1 + k : 2 + k], fresh)
    raw_ref[0:ROWS] = columns_ref[...]
    wide_ref[...] = jnp.zeros((128, 128), F32)
    wide_ref[0:32] = above_ref[8 * STRIP : 8 * STRIP + 32]
    raw_ref[ROWS : 2 * ROWS] = wide_ref[...].T

    @pl.when(slab == 3)
    def _():
        for z in range(CZ):
            raw_ref[ROWS + z * CX : ROWS + (z + 1) * CX] = fresh

    beyond = gather(CX, lambda c: above2_ref[2 * c * CX : (2 * c + 1) * CX])
    raw_ref[2 * ROWS : 2 * ROWS + CX] = jnp.where(slab >= 2, fresh, beyond)

    def rows_at(row):
        return raw_ref[pl.ds(pl.multiple_of(row * CX, CX), CX)]

    flag_lane = (lanes_of(CX) == 24) | (lanes_of(CX) == 25)
    for z in range(CZ):
        wide_ref[z * CX : (z + 1) * CX] = jnp.where(flag_lane, columns_ref[0:CX], rows_at(shift + z))
    out_ref[0:32] = wide_ref[...].T[0:32]
    wide_ref[...] = jnp.zeros((128, 128), F32)
    wide_ref[0:CX] = rows_at(first)
    wide_ref[112:128] = rows_at(last)
    out_ref[32:56] = wide_ref[...].T[0:24]


def pack_y(turned_ref, before_ref, after_ref, out_ref, sides_ref):
    out_ref[0:56] = turned_ref[...]
    sides_ref[...] = jnp.zeros((128, 128), F32)
    sides_ref[pl.ds(0, 8, stride=CX)] = gather(8, lambda c: before_ref[pl.ds(8 + c, 8, stride=8)])
    sides_ref[pl.ds(15, 8, stride=CX)] = gather(8, lambda c: after_ref[pl.ds(8 + c, 8, stride=8)])
    out_ref[56:80] = sides_ref[...].T[0:24]


def read_parameters(stiffness_ref, barrier_ref, coupling_ref, slope_ref, diffusivity_ref, release_ref):
    return dict(
        stiffness=[[stiffness_ref[a, e] for e in range(3)] for a in range(4)],
        barrier=[barrier_ref[a] for a in range(4)],
        coupling=[[coupling_ref[a, k] for k in range(3)] for a in range(4)],
        slope=[slope_ref[a] for a in range(4)],
        base=[0.5 * diffusivity_ref[3, k] for k in range(3)],
        excess=[[0.5 * (diffusivity_ref[a, k] - diffusivity_ref[3, k]) for k in range(3)] for a in range(3)],
        release=[[release_ref[a, k] for k in range(3)] for a in range(4)],
    )


def advance(own, neighbours, flag, height, par):
    fractions = list(own[:3])
    fractions.append(1.0 - (own[0] + own[1] + own[2]))
    solutes = own[3:]

    def half_density(at, k):
        return par["base"][k] + (
            par["excess"][0][k] * at[0] + par["excess"][1][k] * at[1] + par["excess"][2][k] * at[2]
        )

    own_density = [half_density(own, k) for k in range(3)]
    gains = [None] * 3
    laplace = [None] * 4
    for e, (upper, lower) in enumerate(neighbours):
        curve = [upper[a] + lower[a] - 2.0 * own[a] for a in range(3)]
        curve.append(-(curve[0] + curve[1] + curve[2]))
        for a in range(4):
            term = par["stiffness"][a][e] * curve[a]
            laplace[a] = term if laplace[a] is None else laplace[a] + term
        for beside in (upper, lower):
            for k in range(3):
                flow = (own_density[k] + half_density(beside, k)) * (beside[3 + k] - solutes[k])
                gains[k] = flow if gains[k] is None else gains[k] + flow
    rates = []
    for a in range(4):
        p = fractions[a]
        drive = par["slope"][a] * height + par["barrier"][a] * (2.0 * p - 1.0)
        for k in range(3):
            drive = drive + par["coupling"][a][k] * solutes[k]
        rates.append(flag * (laplace[a] + p * (1.0 - p) * drive))
    mean = 0.25 * (rates[0] + rates[1] + rates[2] + rates[3])
    changes = [rate - mean for rate in rates]
    after = [fractions[a] + changes[a] for a in range(4)]
    for k in range(3):
        released = par["release"][0][k] * changes[0]
        for a in range(1, 4):
            released = released + par["release"][a][k] * changes[a]
        after.append(solutes[k] + gains[k] + released)
    return after[:3] + after[4:], after[3]


def steps(
    own_ref, above_ref, above2_ref, below_ref, before_ref, after_ref, own_y_ref, left_ref, right_ref, meta_ref,
    slots_ref, slab_ref,
    stiffness_ref, barrier_ref, coupling_ref, slope_ref, diffusivity_ref, release_ref,
    phases_ref, solutes_ref, send_ref,
    raw_ref, window_ref, edge_ref, turned_ref, first_ref, xface_ref, final_ref,
):
    slab = slab_ref[0]
    at_bottom = slab == 0
    at_top = slab == 3
    par = read_parameters(stiffness_ref, barrier_ref, coupling_ref, slope_ref, diffusivity_ref, release_ref)
    first_row = (slab * CZ).astype(F32)

    def height_of(z):
        return (first_row + z + 0.5) / 32.0 - 0.5

    lane16, lane8, sub16 = lanes_of(CX), lanes_of(8), sublanes_of(CX)
    flags = own_ref[KEPT * ROWS : KEPT * ROWS + CX]

    shift = jnp.max(meta_ref[0:1]).astype(jnp.int32)
    for c in range(KEPT):
        fresh = jnp.zeros((CX, 128), F32) + (meta_ref[c - 2 : c - 1] if c >= 3 else 0.0)
        raw_ref[c, 0:CX] = below_ref[c * CX : (c + 1) * CX]
        raw_ref[c, CX : 9 * CX] = own_ref[c * ROWS : (c + 1) * ROWS]
        for z in range(CZ):
            here = above_ref[c * ROWS + z * CX : c * ROWS + (z + 1) * CX]
            raw_ref[c, (9 + z) * CX : (10 + z) * CX] = jnp.where(at_top, fresh, here)
        for z in range(2):
            here = above2_ref[(2 * c + z) * CX : (2 * c + z + 1) * CX]
            raw_ref[c, (17 + z) * CX : (18 + z) * CX] = jnp.where(slab >= 2, fresh, here)
        for w in range(WINDOW):
            row = shift - 1 + w
            if w == 1:
                row = jnp.where(at_bottom, row + 1, row)
            if w == WINDOW - 2:
                row = jnp.where(at_top, row - 1, row)
            window_ref[c, w * CX : (w + 1) * CX] = raw_ref[c, pl.ds(pl.multiple_of(row * CX, CX), CX)]

    edge_ref[...] = jnp.zeros((128, 128), F32)
    for group, start in ((0, 0), (1, 32), (2, 56)):
        for c in range(KEPT):
            at = group * 12 + 2 * c
            edge_ref[at : at + 1] = right_ref[start + 4 * c + 2 : start + 4 * c + 3]
            edge_ref[at + 1 : at + 2] = left_ref[start + 4 * c + 1 : start + 4 * c + 2]
    turned_ref[...] = edge_ref[...].T

    def beside_y(value, rows, column):
        lane = lane16 if value.shape[0] == CX else lane8
        fill = pltpu.roll(rows, 127 - column, 1)
        upper = jnp.where(lane == 127, fill, pltpu.roll(value, 127, 1))
        lower = jnp.where(lane == 0, fill, pltpu.roll(value, 1, 1))
        return upper, lower

    def beside_x(ref, c, start, low_row, high_row):
        upper = jnp.where(sub16 == 15, high_row, ref[c, start + 1 : start + 1 + CX])
        lower = jnp.where(sub16 == 0, low_row, ref[c, start - 1 : start - 1 + CX])
        return upper, lower

    def split(pairs):
        return ([pair[0] for pair in pairs], [pair[1] for pair in pairs])

    for w in range(1, WINDOW - 1):
        z = w - 2
        start = w * CX
        own = [window_ref[c, start : start + CX] for c in range(KEPT)]
        along_z = (
            [window_ref[c, start + CX : start + 2 * CX] for c in range(KEPT)],
            [window_ref[c, start - CX : start] for c in range(KEPT)],
        )
        along_x = split(
            [
                beside_x(
                    window_ref, c, start,
                    before_ref[(z + 1) * 8 + c : (z + 1) * 8 + c + 1],
                    after_ref[(z + 1) * 8 + c : (z + 1) * 8 + c + 1],
                )
                for c in range(KEPT)
            ]
        )
        if z == -1:
            rows, group, flag = turned_ref[0:CX], 1, below_ref[KEPT * CX : (KEPT + 1) * CX]
        elif z == CZ:
            rows, group, flag = turned_ref[112:128], 1, above_ref[KEPT * ROWS : KEPT * ROWS + CX]
        else:
            rows, group, flag = turned_ref[z * CX : (z + 1) * CX], 0, flags
        along_y = split([beside_y(own[c], rows, group * 12 + 2 * c) for c in range(KEPT)])
        result, _ = advance(own, (along_z, along_x, along_y), flag, height_of(z), par)
        for c in range(KEPT):
            first_ref[c, (w - 1) * CX : w * CX] = result[c]

    @pl.when(at_bottom)
    def _():
        for c in range(KEPT):
            first_ref[c, 0:CX] = first_ref[c, CX : 2 * CX]

    @pl.when(at_top)
    def _():
        for c in range(KEPT):
            first_ref[c, 9 * CX : 10 * CX] = first_ref[c, 8 * CX : 9 * CX]

    face_height = height_of(sublanes_of(8).astype(F32))
    for side, ref, x in ((0, before_ref, 0), (1, after_ref, 15)):
        own = [ref[pl.ds(8 + c, 8, stride=8)] for c in range(KEPT)]
        along_z = (
            [ref[pl.ds(16 + c, 8, stride=8)] for c in range(KEPT)],
            [ref[pl.ds(c, 8, stride=8)] for c in range(KEPT)],
        )
        along_x = (
            [ref[pl.ds(FAR + c, 8, stride=8)] for c in range(KEPT)],
            [window_ref[c, pl.ds(2 * CX + x, 8, stride=CX)] for c in range(KEPT)],
        )
        rows = turned_ref[pl.ds(x, 8, stride=CX)]
        along_y = split([beside_y(own[c], rows, 24 + 2 * c) for c in range(KEPT)])
        flag = ref[KEPT : KEPT + 1]
        result, _ = advance(own, (along_z, along_x, along_y), flag, face_height, par)
        for c in range(KEPT):
            xface_ref[side * KEPT + c] = result[c]

    sub8 = sublanes_of(8)

    def both(right_row, left_row):
        return jnp.where(sub8 == 0, right_row, left_row)

    def lifted(c, start):
        return both(
            right_ref[start + 4 * c + 2 : start + 4 * c + 3],
            left_ref[start + 4 * c + 1 : start + 4 * c + 2],
        )

    own = [lifted(c, 0) for c in range(KEPT)]
    ends = [lifted(c, 32) for c in range(KEPT)]
    sides = [lifted(c, 56) for c in range(KEPT)]
    outer = [both(right_ref[4 * c + 3 : 4 * c + 4], left_ref[4 * c : 4 * c + 1]) for c in range(KEPT)]
    inner = [both(own_y_ref[4 * c + 1 : 4 * c + 2], own_y_ref[4 * c + 2 : 4 * c + 3]) for c in range(KEPT)]
    along_z = (
        [jnp.where(lane8 >= 112, ends[c], pltpu.roll(own[c], 112, 1)) for c in range(KEPT)],
        [jnp.where(lane8 < 16, ends[c], pltpu.roll(own[c], 16, 1)) for c in range(KEPT)],
    )
    along_x = (
        [jnp.where(lane8 % 16 == 15, sides[c], pltpu.roll(own[c], 127, 1)) for c in range(KEPT)],
        [jnp.where(lane8 % 16 == 0, sides[c], pltpu.roll(own[c], 1, 1)) for c in range(KEPT)],
    )
    flag = both(right_ref[25:26], left_ref[24:25])
    result, _ = advance(
        own, (along_z, along_x, (outer, inner)), flag, height_of((lane8 // 16).astype(F32)), par
    )
    for c in range(KEPT):
        edge_ref[2 * c : 2 * c + 2] = result[c][0:2]
    turned_ref[...] = edge_ref[...].T

    for z in range(CZ):
        start = (z + 1) * CX
        own = [first_ref[c, start : start + CX] for c in range(KEPT)]
        along_z = (
            [first_ref[c, start + CX : start + 2 * CX] for c in range(KEPT)],
            [first_ref[c, start - CX : start] for c in range(KEPT)],
        )
        along_x = split(
            [
                beside_x(first_ref, c, start, xface_ref[c, z : z + 1], xface_ref[KEPT + c, z : z + 1])
                for c in range(KEPT)
            ]
        )
        rows = turned_ref[z * CX : (z + 1) * CX]
        along_y = split([beside_y(own[c], rows, 2 * c) for c in range(KEPT)])
        result, last = advance(own, (along_z, along_x, along_y), flags, height_of(z), par)
        for c in range(3):
            phases_ref[c, z * CX : (z + 1) * CX] = result[c]
            solutes_ref[c, z * CX : (z + 1) * CX] = result[3 + c]
        phases_ref[3, z * CX : (z + 1) * CX] = last
        for c in range(KEPT):
            final_ref[c * ROWS + z * CX : c * ROWS + (z + 1) * CX] = result[c]

    for owner in range(64):
        send_ref[owner, 0:1] = jnp.full((1, 128), MARKER, F32)
    group = lane8 // 8
    for b in range(2):
        for q in range(4):
            parts = []
            for i in range(16):
                row = (2 * q + i // 8) * CX + b * 8 + i % 8
                parts.append(final_ref[pl.ds(row, 8, stride=ROWS)])
            for step in (8, 4, 2, 1):
                keep = (group & step) == 0
                swapped = list(parts)
                for i in range(16):
                    if i & step == 0:
                        one, two = parts[i], parts[i + step]
                        swapped[i] = jnp.where(keep, one, pltpu.roll(two, step * 8, 1))
                        swapped[i + step] = jnp.where(keep, pltpu.roll(one, 128 - step * 8, 1), two)
                parts = swapped
            for d in range(16):
                slot = slots_ref[b * 16 + d]
                send_ref[slot >> 1, pl.ds(2 * q + (slot & 1), KEPT, stride=8)] = parts[d][0:6]


def place(arrived_ref, moved_ref, sources):
    sub16 = sublanes_of(16)
    weight = jnp.zeros((16, 128), F32)
    for i in range(16):
        weight = jnp.where((sub16 == i) & (lanes_of(16) == 0), float(2**i), weight)
    masks = []
    for block in range(4):
        first = jnp.concatenate([arrived_ref[block * 16 + i, 0:1] for i in range(16)], axis=0)
        masks.append(jnp.sum(jnp.where(first < LIMIT, weight, 0.0)).astype(jnp.int32))
    count = jnp.int32(0)
    for source in range(64):
        sources[count] = source
        count = count + ((masks[source // 16] >> (source % 16)) & 1)
    for n in range(0, 16, 4):
        group = [sources[n + i] & 63 for i in range(4)]
        rows = slice(2 * n, 2 * n + 8)
        for q in range(4):
            span = slice(q * 128, (q + 1) * 128)
            parts = []
            for c in range(KEPT):
                at = 8 * c + 2 * q
                parts.append(jnp.concatenate([arrived_ref[s, at : at + 2] for s in group], axis=0))
            for c in range(3):
                moved_ref[c, rows, span] = parts[c]
                moved_ref[4 + c, rows, span] = parts[3 + c]
            moved_ref[3, rows, span] = 1.0 - (parts[0] + parts[1] + parts[2])


def shape_of(*dims):
    return jax.ShapeDtypeStruct(dims, F32)


PARAMS = pltpu.CompilerParams(vmem_limit_bytes=32 * 1024 * 1024)


def call(body, ins, outs, scratch=(), flops=0):
    return pl.pallas_call(
        body,
        in_specs=list(ins),
        out_specs=[VMEM] * len(outs),
        out_shape=list(outs),
        scratch_shapes=list(scratch),
        compiler_params=PARAMS,
        cost_estimate=pl.CostEstimate(flops=flops, bytes_accessed=1000000, transcendentals=0),
    )


def shifted(value, axis, by, wrap):
    count = lax.axis_size(axis)
    pairs = [
        (source, (source + by) % count) for source in range(count) if wrap or 0 <= source + by < count
    ]
    return lax.ppermute(value, axis, pairs)


def per_device(
    phases, solutes, melt, shift_rows, flags, balance,
    stiffness, barrier, coupling, slope, diffusivity, release,
):
    slab = lax.axis_index("gz").astype(jnp.int32).reshape(1)
    owner_list = balance.reshape(32)
    serial = jnp.arange(32)
    earlier = jnp.sum(
        ((owner_list[:, None] == owner_list[None, :]) & (serial[None, :] < serial[:, None])).astype(jnp.int32),
        axis=1,
    )
    slots = owner_list * 2 + earlier

    bulk, second, last, strip, columns, meta = call(
        pack_z,
        [ANY] * 5,
        [
            shape_of(KEPT * ROWS + CX, 128), shape_of(KEPT * 2 * CX, 128), shape_of((KEPT + 1) * CX, 128),
            shape_of(8 * STRIP + 32, 128), shape_of(ROWS, 128), shape_of(8, 128),
        ],
        [
            pltpu.SMEM((1, 1, 1, 32), jnp.int32), pltpu.SMEM((1,), jnp.int32), pltpu.SMEM((3,), F32),
            pltpu.SemaphoreType.DMA((KEPT,)), pltpu.SemaphoreType.DMA((3,)),
        ],
    )(phases.reshape(4, ROWS, CY), solutes.reshape(3, ROWS, CY), flags, shift_rows, melt)
    above_strip = shifted(strip, "gz", -1, False)
    above2 = shifted(second, "gz", -2, False)
    below = shifted(last, "gz", 1, False)
    late_bulk, _ = lax.optimization_barrier((bulk, above_strip))
    above = shifted(late_bulk, "gz", -1, False)

    low, high = call(
        pack_x,
        [VMEM] * 5 + [SMEM],
        [shape_of(FAR + 64, 128)] * 2,
        [pltpu.VMEM((17 * STRIP, 128), F32)],
    )(strip, above_strip, above2, bulk, meta, slab)
    before = shifted(high, "gx", 1, True)
    after = shifted(low, "gx", -1, True)

    (turned,) = call(
        turn_columns,
        [VMEM] * 4 + [SMEM],
        [shape_of(56, 128)],
        [pltpu.VMEM((17 * CX, 128), F32), pltpu.VMEM((128, 128), F32)],
    )(columns, above_strip, above2, meta, slab)
    (faces,) = call(pack_y, [VMEM] * 3, [shape_of(80, 128)], [pltpu.VMEM((128, 128), F32)])(
        turned, before, after
    )
    left = shifted(faces, "gy", 1, True)
    right = shifted(faces, "gy", -1, True)

    phases_out, solutes_out, send = call(
        steps,
        [VMEM] * 10 + [SMEM] * 8,
        [shape_of(4, ROWS, CY), shape_of(3, ROWS, CY), shape_of(64, 48, 128)],
        [
            pltpu.VMEM((KEPT, 19 * CX, 128), F32),
            pltpu.VMEM((KEPT, WINDOW * CX, 128), F32),
            pltpu.VMEM((128, 128), F32),
            pltpu.VMEM((128, 128), F32),
            pltpu.VMEM((KEPT, 10 * CX, 128), F32),
            pltpu.VMEM((2 * KEPT, 8, 128), F32),
            pltpu.VMEM((8 * ROWS, 128), F32),
        ],
    )(
        bulk, above, above2, below, before, after, faces, left, right, meta, slots, slab,
        stiffness, barrier, coupling, slope, diffusivity, release,
    )
    arrived = lax.all_to_all(send, ("gx", "gy"), split_axis=0, concat_axis=0, tiled=True)
    (moved,) = call(place, [VMEM], [shape_of(7, 32, 512)], [pltpu.SMEM((65,), jnp.int32)])(arrived)
    return (
        phases_out.reshape(4, CZ, CX, CY),
        solutes_out.reshape(3, CZ, CX, CY),
        jnp.transpose(moved, (1, 0, 2)),
    )


def solution(mesh):
    block = P(None, "gz", "gx", "gy")
    table = P("gz", "gx", "gy", None)
    return jax.shard_map(
        per_device,
        mesh=mesh,
        in_specs=(block, block, P(), P(), table, table, P(), P(), P(), P(), P(), P()),
        out_specs=(block, block, P(("gz", "gx", "gy"), None, None)),
        check_vma=False,
    )
```

```python
import jax
import jax.numpy as jnp
from jax import lax
from jax.experimental import pallas as pl
from jax.experimental.pallas import tpu as pltpu
from jax.sharding import PartitionSpec as P

CZ, CX, CY = 8, 16, 128
KEPT = 6
HELD = KEPT + 3
WINDOW = CZ + 4
ROWS = CZ * CX
X_ROWS = 18
MARKER = 3.0e38
LIMIT = 1.0e30
F32 = jnp.float32

VMEM = pl.BlockSpec(memory_space=pltpu.VMEM)
SMEM = pl.BlockSpec(memory_space=pltpu.SMEM)


def lanes_of(rows):
    return lax.broadcasted_iota(jnp.int32, (rows, 128), 1)


def sublanes_of(rows):
    return lax.broadcasted_iota(jnp.int32, (rows, 128), 0)


def flag_row(small_ref, b):
    group = lanes_of(8) // 8
    row = jnp.zeros((8, 128), F32)
    for d in range(16):
        row = jnp.where(group == d, small_ref[b * 16 + d].astype(F32), row)
    return row


LAYERS = (0, 1, 14, 15)
STRIP = 24
PAIRED = 8 * STRIP + 32


def gather(rows, value_of):
    lane = lanes_of(rows)
    packed = jnp.zeros((rows, 128), F32)
    for c in range(KEPT):
        moved = pltpu.roll(value_of(c), 2 + 4 * c, 1)
        packed = jnp.where((lane >= 4 * c) & (lane < 4 * c + 4), moved, packed)
    return packed


def pack_z(
    phases_ref, solutes_ref, small_ref, slab_ref,
    bulk_ref, second_ref, early_ref, even_ref, odd_ref, strip_ref, columns_ref, meta_ref,
    last_ref,
):
    flags = jnp.concatenate([flag_row(small_ref, b) for b in range(2)], axis=0)
    bulk_ref[KEPT * ROWS : KEPT * ROWS + CX] = flags
    last_ref[KEPT * CX : (KEPT + 1) * CX] = flags
    meta_ref[0:8] = jnp.full((8, 128), small_ref[32].astype(F32), F32)
    meta_ref[8:24] = flags
    for c in range(KEPT):
        source = phases_ref.at[c] if c < 3 else solutes_ref.at[c - 3]
        bulk_ref[c * ROWS : (c + 1) * ROWS] = source[...]
        second_ref[2 * c * CX : 2 * (c + 1) * CX] = bulk_ref[c * ROWS : c * ROWS + 2 * CX]
        last_ref[c * CX : (c + 1) * CX] = bulk_ref[c * ROWS + 7 * CX : (c + 1) * ROWS]
        for n, x in enumerate(LAYERS):
            strip_ref[pl.ds(n * KEPT + c, 8, stride=STRIP)] = bulk_ref[pl.ds(c * ROWS + x, 8, stride=CX)]
            early_ref[n * KEPT + c : n * KEPT + c + 1] = bulk_ref[c * ROWS + x : c * ROWS + x + 1]
    flags = pltpu.roll(flags, 25, 1)
    flag_lane = (lanes_of(CX) == 24) | (lanes_of(CX) == 25)
    for z in range(CZ):
        packed = gather(CX, lambda c: bulk_ref[c * ROWS + z * CX : c * ROWS + (z + 1) * CX])
        columns_ref[z * CX : (z + 1) * CX] = jnp.where(flag_lane, flags, packed)
    early_ref[STRIP : STRIP + CX] = columns_ref[0:CX]
    strip_ref[8 * STRIP : PAIRED] = columns_ref[...].T[0:32]
    is_even = (slab_ref[0] & 1) == 0
    last_ref[(KEPT + 1) * CX : PAIRED] = jnp.zeros((PAIRED - (KEPT + 1) * CX, 128), F32)
    even_ref[...] = jnp.where(is_even, last_ref[...], strip_ref[...])
    odd_ref[...] = jnp.where(is_even, strip_ref[...], last_ref[...])


def melt_of(row_ref, k):
    row = row_ref[...]
    lane = lax.broadcasted_iota(jnp.int32, row.shape, 1)
    return jnp.sum(jnp.where(lane == k, row, 0.0), axis=1, keepdims=True)


def window_ends(meta_ref, slab_ref):
    shift = jnp.max(meta_ref[0:1]).astype(jnp.int32)
    slab = slab_ref[0]
    return shift, jnp.where(slab == 0, shift, shift - 1), jnp.where(slab == 3, shift + 7, shift + 8)


def pack_x(own_ref, even_ref, odd_ref, above2_ref, meta_ref, row_ref, slab_ref, low_ref, high_ref, raw_ref):
    slab = slab_ref[0]
    shift, first, last = window_ends(meta_ref, slab_ref)
    fresh = jnp.zeros((STRIP, 128), F32)
    sub = sublanes_of(STRIP) % KEPT
    for k in range(3):
        fresh = jnp.where(sub == 3 + k, melt_of(row_ref, k), fresh)
    raw_ref[0 : 8 * STRIP] = own_ref[0 : 8 * STRIP]
    for z in range(CZ):
        rows = slice(z * STRIP, (z + 1) * STRIP)
        here = jnp.where((slab & 1) == 0, even_ref[rows], odd_ref[rows])
        raw_ref[(8 + z) * STRIP : (9 + z) * STRIP] = jnp.where(slab == 3, fresh, here)
    raw_ref[16 * STRIP : 17 * STRIP] = above2_ref[0:STRIP]

    @pl.when(slab >= 2)
    def _():
        raw_ref[16 * STRIP : 17 * STRIP] = fresh

    for i in range(10):
        row = first if i == 0 else last if i == 9 else shift + (i - 1)
        value = raw_ref[pl.ds(pl.multiple_of(row * STRIP, 8), STRIP)]
        low_ref[pl.ds(i, KEPT, stride=X_ROWS)] = value[0:6]
        high_ref[pl.ds(i, KEPT, stride=X_ROWS)] = value[18:24]
        if 0 < i < 9:
            low_ref[pl.ds(9 + i, KEPT, stride=X_ROWS)] = value[6:12]
            high_ref[pl.ds(9 + i, KEPT, stride=X_ROWS)] = value[12:18]
    flags = meta_ref[8:24]
    low_ref[KEPT * X_ROWS : KEPT * X_ROWS + 4] = flags[0:4]
    high_ref[KEPT * X_ROWS : KEPT * X_ROWS + 4] = flags[12:16]


def turn_columns(
    columns_ref, even_ref, odd_ref, above2_ref, meta_ref, row_ref, slab_ref, balance_ref,
    out_ref, slots_ref, raw_ref, wide_ref, given_ref,
):
    for owner in range(64):
        given_ref[owner] = jnp.int32(0)
    for t in range(32):
        owner = balance_ref[0, 0, 0, t]
        slots_ref[t] = 2 * owner + given_ref[owner]
        given_ref[owner] = jnp.int32(1)

    slab = slab_ref[0]
    shift, first, last = window_ends(meta_ref, slab_ref)
    fresh = jnp.zeros((CX, 128), F32)
    part = lanes_of(CX) // 4
    for k in range(3):
        fresh = jnp.where(part == 3 + k, melt_of(row_ref, k), fresh)
    raw_ref[0:ROWS] = columns_ref[...]
    wide_ref[...] = jnp.zeros((128, 128), F32)
    wide_ref[0:32] = jnp.where((slab & 1) == 0, even_ref[8 * STRIP : PAIRED], odd_ref[8 * STRIP : PAIRED])
    raw_ref[ROWS : 2 * ROWS] = wide_ref[...].T

    @pl.when(slab == 3)
    def _():
        for z in range(CZ):
            raw_ref[ROWS + z * CX : ROWS + (z + 1) * CX] = fresh

    raw_ref[2 * ROWS : 2 * ROWS + CX] = jnp.where(slab >= 2, fresh, above2_ref[STRIP : STRIP + CX])

    def rows_at(row):
        return raw_ref[pl.ds(pl.multiple_of(row * CX, CX), CX)]

    flag_lane = (lanes_of(CX) == 24) | (lanes_of(CX) == 25)
    for z in range(CZ):
        wide_ref[z * CX : (z + 1) * CX] = jnp.where(flag_lane, columns_ref[0:CX], rows_at(shift + z))
    out_ref[0:32] = wide_ref[...].T[0:32]
    wide_ref[...] = jnp.zeros((128, 128), F32)
    wide_ref[0:CX] = rows_at(first)
    wide_ref[112:128] = rows_at(last)
    out_ref[32:56] = wide_ref[...].T[0:24]


def pack_y(turned_ref, before_ref, after_ref, up_ref, down_ref, sides_ref):
    sides_ref[...] = jnp.zeros((128, 128), F32)
    sides_ref[pl.ds(0, 8, stride=CX)] = gather(8, lambda c: before_ref[c * X_ROWS + 1 : c * X_ROWS + 9])
    sides_ref[pl.ds(15, 8, stride=CX)] = gather(8, lambda c: after_ref[c * X_ROWS + 1 : c * X_ROWS + 9])
    sides_ref[...] = sides_ref[...].T
    for ref, near, far in ((up_ref, 1, 0), (down_ref, 2, 3)):
        ref[0:6] = turned_ref[pl.ds(near, KEPT, stride=4)]
        ref[6:12] = turned_ref[pl.ds(far, KEPT, stride=4)]
        ref[12:18] = turned_ref[pl.ds(32 + near, KEPT, stride=4)]
        ref[18:24] = sides_ref[pl.ds(near, KEPT, stride=4)]
        ref[24:25] = turned_ref[23 + near : 24 + near]


def read_parameters(table_ref, plain_ref):
    stiffness = [[table_ref[a, e] for e in range(3)] for a in range(4)]
    return dict(
        stiffness=stiffness,
        total=[row[0] + row[1] + row[2] for row in stiffness],
        coupling=[[table_ref[a, 3 + k] for k in range(3)] for a in range(4)],
        base=[0.5 * table_ref[3, 6 + k] for k in range(3)],
        excess=[[0.5 * (table_ref[a, 6 + k] - table_ref[3, 6 + k]) for k in range(3)] for a in range(3)],
        release=[[table_ref[a, 9 + k] for k in range(3)] for a in range(4)],
        barrier=[plain_ref[3 + a] for a in range(4)],
        twice=[2.0 * plain_ref[3 + a] for a in range(4)],
        slope=[plain_ref[7 + a] for a in range(4)],
    )


def with_densities(kept_values, par):
    p = kept_values[:3]
    return list(kept_values) + [
        par["base"][k] + (par["excess"][0][k] * p[0] + par["excess"][1][k] * p[1] + par["excess"][2][k] * p[2])
        for k in range(3)
    ]


def flows(own, beside):
    return [(own[6 + k] + beside[6 + k]) * (beside[3 + k] - own[3 + k]) for k in range(3)]


def advance(own, neighbours, flag, height, par, flow_below=None):
    others = own[0] + own[1] + own[2]
    fractions = [own[0], own[1], own[2], 1.0 - others]
    solutes = own[3:6]
    stiffness = par["stiffness"]
    total = par["total"]
    laplace = [(-2.0 * total[a]) * own[a] for a in range(3)] + [(2.0 * total[3]) * others]
    gains = None
    flow_above = None
    for e, (upper, lower) in enumerate(neighbours):
        sums = [upper[a] + lower[a] for a in range(3)]
        for a in range(3):
            laplace[a] = laplace[a] + stiffness[a][e] * sums[a]
        laplace[3] = laplace[3] - stiffness[3][e] * (sums[0] + sums[1] + sums[2])
        gained = flows(own, upper)
        if e == 0:
            flow_above = gained
        if e == 0 and flow_below is not None:
            gained = [gained[k] - flow_below[k] for k in range(3)]
        else:
            more = flows(own, lower)
            gained = [gained[k] + more[k] for k in range(3)]
        gains = gained if e == 0 else [gains[k] + gained[k] for k in range(3)]
    rates = []
    for a in range(4):
        p = fractions[a]
        drive = (par["slope"][a] * height - par["barrier"][a]) + par["twice"][a] * p
        for k in range(3):
            drive = drive + par["coupling"][a][k] * solutes[k]
        rates.append(flag * (laplace[a] + (p - p * p) * drive))
    mean = 0.25 * ((rates[0] + rates[1]) + (rates[2] + rates[3]))
    changes = [rate - mean for rate in rates]
    after = [fractions[a] + changes[a] for a in range(4)]
    for k in range(3):
        released = par["release"][0][k] * changes[0]
        for a in range(1, 4):
            released = released + par["release"][a][k] * changes[a]
        after.append(solutes[k] + (gains[k] + released))
    return after[:3] + after[4:], after[3], flow_above


def steps(
    own_ref, above_ref, above2_ref, even_ref, odd_ref, before_ref, after_ref, own_y_ref, left_ref, right_ref, meta_ref,
    slots_ref, slab_ref, plain_ref, table_ref,
    phases_ref, solutes_ref, send_ref,
    raw_ref, window_ref, edge_ref, turned_ref, first_ref, side_ref, xface_ref, final_ref,
):
    slab = slab_ref[0]
    at_bottom = slab == 0
    at_top = slab == 3
    par = read_parameters(table_ref, plain_ref)
    first_row = (slab * CZ).astype(F32)

    def height_of(z):
        return (first_row + z + 0.5) / 32.0 - 0.5

    lane16, lane8, sub16 = lanes_of(CX), lanes_of(8), sublanes_of(CX)
    flags = own_ref[KEPT * ROWS : KEPT * ROWS + CX]

    def below(c):
        rows = slice(c * CX, (c + 1) * CX)
        return jnp.where((slab & 1) == 0, odd_ref[rows], even_ref[rows])

    shift = jnp.max(meta_ref[0:1]).astype(jnp.int32)
    for c in range(KEPT):
        fresh = jnp.full((CX, 128), plain_ref[c - 3] if c >= 3 else 0.0, F32)
        raw_ref[c, 0:CX] = below(c)
        raw_ref[c, CX : 9 * CX] = own_ref[c * ROWS : (c + 1) * ROWS]
        for z in range(CZ):
            here = above_ref[c * ROWS + z * CX : c * ROWS + (z + 1) * CX]
            raw_ref[c, (9 + z) * CX : (10 + z) * CX] = jnp.where(at_top, fresh, here)
        for z in range(2):
            here = above2_ref[(2 * c + z) * CX : (2 * c + z + 1) * CX]
            raw_ref[c, (17 + z) * CX : (18 + z) * CX] = jnp.where(slab >= 2, fresh, here)
        for w in range(WINDOW):
            row = shift - 1 + w
            if w == 1:
                row = jnp.where(at_bottom, row + 1, row)
            if w == WINDOW - 2:
                row = jnp.where(at_top, row - 1, row)
            window_ref[c, w * CX : (w + 1) * CX] = raw_ref[c, pl.ds(pl.multiple_of(row * CX, CX), CX)]

    for w in range(WINDOW):
        rows = slice(w * CX, (w + 1) * CX)
        held = with_densities([window_ref[c, rows] for c in range(KEPT)], par)
        for c in range(KEPT, HELD):
            window_ref[c, rows] = held[c]
    for side, ref in ((0, before_ref), (1, after_ref)):
        held = with_densities([ref[c * X_ROWS : (c + 1) * X_ROWS] for c in range(KEPT)], par)
        for c in range(HELD):
            side_ref[side * HELD + c, 0:X_ROWS] = held[c]

    edge_ref[...] = jnp.zeros((128, 128), F32)
    for group, start in ((0, 0), (1, 12), (2, 18)):
        for ref, odd_row in ((right_ref, 0), (left_ref, 1)):
            held = with_densities([ref[start + c : start + c + 1] for c in range(KEPT)], par)
            for c in range(HELD):
                at = group * 2 * HELD + 2 * c + odd_row
                edge_ref[at : at + 1] = held[c]
    turned_ref[...] = edge_ref[...].T

    def beside_y(value, rows, column):
        lane = lane16 if value.shape[0] == CX else lane8
        fill = pltpu.roll(rows, 127 - column, 1)
        upper = jnp.where(lane == 127, fill, pltpu.roll(value, 127, 1))
        lower = jnp.where(lane == 0, fill, pltpu.roll(value, 1, 1))
        return upper, lower

    def beside_x(ref, c, start, low_row, high_row):
        upper = jnp.where(sub16 == 15, high_row, ref[c, start + 1 : start + 1 + CX])
        lower = jnp.where(sub16 == 0, low_row, ref[c, start - 1 : start - 1 + CX])
        return upper, lower

    def split(pairs):
        return ([pair[0] for pair in pairs], [pair[1] for pair in pairs])

    def store_held(ref, rows, values):
        for c, value in enumerate(with_densities(values, par)):
            ref[c, rows] = value

    flow = None
    for w in range(1, WINDOW - 1):
        z = w - 2
        start = w * CX
        own = [window_ref[c, start : start + CX] for c in range(HELD)]
        along_z = (
            [window_ref[c, start + CX : start + 2 * CX] for c in range(HELD)],
            [window_ref[c, start - CX : start] for c in range(HELD)],
        )
        along_x = split(
            [
                beside_x(
                    window_ref, c, start,
                    side_ref[c, z + 1 : z + 2], side_ref[HELD + c, z + 1 : z + 2],
                )
                for c in range(HELD)
            ]
        )
        if z == -1:
            rows, group, flag = turned_ref[0:CX], 1, below(KEPT)
        elif z == CZ:
            rows, group, flag = turned_ref[112:128], 1, above_ref[KEPT * ROWS : KEPT * ROWS + CX]
        else:
            rows, group, flag = turned_ref[z * CX : (z + 1) * CX], 0, flags
        along_y = split([beside_y(own[c], rows, 2 * (group * HELD + c)) for c in range(HELD)])
        result, _, flow = advance(own, (along_z, along_x, along_y), flag, height_of(z), par, flow)
        store_held(first_ref, slice((w - 1) * CX, w * CX), result)

    @pl.when(at_bottom)
    def _():
        for c in range(HELD):
            first_ref[c, 0:CX] = first_ref[c, CX : 2 * CX]

    @pl.when(at_top)
    def _():
        for c in range(HELD):
            first_ref[c, 9 * CX : 10 * CX] = first_ref[c, 8 * CX : 9 * CX]

    face_height = height_of(sublanes_of(8).astype(F32))
    for side, ref, x in ((0, before_ref, 0), (1, after_ref, 15)):
        layers = [side_ref.at[side * HELD + c] for c in range(HELD)]
        own = [layer[1:9] for layer in layers]
        along_z = ([layer[2:10] for layer in layers], [layer[0:8] for layer in layers])
        along_x = (
            [layer[10:18] for layer in layers],
            [window_ref[c, pl.ds(2 * CX + x, 8, stride=CX)] for c in range(HELD)],
        )
        rows = turned_ref[pl.ds(x, 8, stride=CX)]
        along_y = split([beside_y(own[c], rows, 2 * (2 * HELD + c)) for c in range(HELD)])
        at = KEPT * X_ROWS + (3 if side == 0 else 0)
        flag = ref[at : at + 1]
        result, _, _ = advance(own, (along_z, along_x, along_y), flag, face_height, par)
        for c, value in enumerate(with_densities(result, par)):
            xface_ref[side * HELD + c] = value

    sub8 = sublanes_of(8)

    def both(right_row, left_row):
        return jnp.where(sub8 == 0, right_row, left_row)

    def lifted(c, start):
        return both(right_ref[start + c : start + c + 1], left_ref[start + c : start + c + 1])

    own, ends, sides, outer = [
        with_densities([lifted(c, start) for c in range(KEPT)], par) for start in (0, 12, 18, 6)
    ]
    inner = with_densities(
        [both(own_y_ref[4 * c + 1 : 4 * c + 2], own_y_ref[4 * c + 2 : 4 * c + 3]) for c in range(KEPT)], par
    )
    along_z = (
        [jnp.where(lane8 >= 112, ends[c], pltpu.roll(own[c], 112, 1)) for c in range(HELD)],
        [jnp.where(lane8 < 16, ends[c], pltpu.roll(own[c], 16, 1)) for c in range(HELD)],
    )
    along_x = (
        [jnp.where(lane8 % 16 == 15, sides[c], pltpu.roll(own[c], 127, 1)) for c in range(HELD)],
        [jnp.where(lane8 % 16 == 0, sides[c], pltpu.roll(own[c], 1, 1)) for c in range(HELD)],
    )
    flag = both(right_ref[24:25], left_ref[24:25])
    result, _, _ = advance(
        own, (along_z, along_x, (outer, inner)), flag, height_of((lane8 // 16).astype(F32)), par
    )
    for c, value in enumerate(with_densities(result, par)):
        edge_ref[2 * c : 2 * c + 2] = value[0:2]
    turned_ref[...] = edge_ref[...].T

    flow = None
    for z in range(CZ):
        start = (z + 1) * CX
        own = [first_ref[c, start : start + CX] for c in range(HELD)]
        along_z = (
            [first_ref[c, start + CX : start + 2 * CX] for c in range(HELD)],
            [first_ref[c, start - CX : start] for c in range(HELD)],
        )
        along_x = split(
            [
                beside_x(first_ref, c, start, xface_ref[c, z : z + 1], xface_ref[HELD + c, z : z + 1])
                for c in range(HELD)
            ]
        )
        rows = turned_ref[z * CX : (z + 1) * CX]
        along_y = split([beside_y(own[c], rows, 2 * c) for c in range(HELD)])
        result, last, flow = advance(own, (along_z, along_x, along_y), flags, height_of(z), par, flow)
        for c in range(3):
            phases_ref[c, z * CX : (z + 1) * CX] = result[c]
            solutes_ref[c, z * CX : (z + 1) * CX] = result[3 + c]
        phases_ref[3, z * CX : (z + 1) * CX] = last
        for c in range(KEPT):
            final_ref[c * ROWS + z * CX : c * ROWS + (z + 1) * CX] = result[c]

    for owner in range(64):
        send_ref[owner, 0:1] = jnp.full((1, 128), MARKER, F32)
    group = lane8 // 8
    for b in range(2):
        for q in range(4):
            parts = []
            for i in range(16):
                row = (2 * q + i // 8) * CX + b * 8 + i % 8
                parts.append(final_ref[pl.ds(row, 8, stride=ROWS)])
            for step in (8, 4, 2, 1):
                keep = (group & step) == 0
                swapped = list(parts)
                for i in range(16):
                    if i & step == 0:
                        one, two = parts[i], parts[i + step]
                        swapped[i] = jnp.where(keep, one, pltpu.roll(two, step * 8, 1))
                        swapped[i + step] = jnp.where(keep, pltpu.roll(one, 128 - step * 8, 1), two)
                parts = swapped
            for d in range(16):
                slot = slots_ref[b * 16 + d]
                send_ref[slot >> 1, pl.ds(2 * q + (slot & 1), KEPT, stride=8)] = parts[d][0:6]


def place(arrived_ref, moved_ref, sources):
    sub16 = sublanes_of(16)
    weight = jnp.zeros((16, 128), F32)
    for i in range(16):
        weight = jnp.where((sub16 == i) & (lanes_of(16) == 0), float(2**i), weight)
    masks = []
    for block in range(4):
        first = jnp.concatenate([arrived_ref[block * 16 + i, 0:1] for i in range(16)], axis=0)
        masks.append(jnp.sum(jnp.where(first < LIMIT, weight, 0.0)).astype(jnp.int32))
    count = jnp.int32(0)
    for source in range(64):
        sources[count] = source
        count = count + ((masks[source // 16] >> (source % 16)) & 1)
    for n in range(0, 16, 4):
        group = [sources[n + i] & 63 for i in range(4)]
        rows = slice(2 * n, 2 * n + 8)
        for q in range(4):
            span = slice(q * 128, (q + 1) * 128)
            parts = []
            for c in range(KEPT):
                at = 8 * c + 2 * q
                parts.append(jnp.concatenate([arrived_ref[s, at : at + 2] for s in group], axis=0))
            for c in range(3):
                moved_ref[c, rows, span] = parts[c]
                moved_ref[4 + c, rows, span] = parts[3 + c]
            moved_ref[3, rows, span] = 1.0 - (parts[0] + parts[1] + parts[2])


def shape_of(*dims):
    return jax.ShapeDtypeStruct(dims, F32)


PARAMS = pltpu.CompilerParams(vmem_limit_bytes=32 * 1024 * 1024)


def call(body, ins, outs, scratch=(), out_specs=None):
    return pl.pallas_call(
        body,
        in_specs=list(ins),
        out_specs=out_specs or [VMEM] * len(outs),
        out_shape=list(outs),
        scratch_shapes=list(scratch),
        compiler_params=PARAMS,
        cost_estimate=pl.CostEstimate(flops=0, bytes_accessed=1000000, transcendentals=0),
    )


def shifted(value, axis, by, wrap):
    count = lax.axis_size(axis)
    pairs = [
        (source, (source + by) % count) for source in range(count) if wrap or 0 <= source + by < count
    ]
    return lax.ppermute(value, axis, pairs)


def per_device(
    phases, solutes, melt, shift_rows, flags, balance,
    stiffness, barrier, coupling, slope, diffusivity, release,
):
    slab = lax.axis_index("gz").astype(jnp.int32).reshape(1)
    small = jnp.concatenate([flags.reshape(32), shift_rows])
    plain = jnp.concatenate([melt, barrier, slope])
    table = jnp.concatenate([stiffness, coupling, diffusivity, release], axis=1)
    bulk, second, early, even, odd, strip, columns, meta = call(
        pack_z,
        [VMEM] * 2 + [SMEM] * 2,
        [
            shape_of(KEPT * ROWS + CX, 128), shape_of(KEPT * 2 * CX, 128), shape_of(STRIP + CX, 128),
            shape_of(PAIRED, 128), shape_of(PAIRED, 128), shape_of(PAIRED, 128), shape_of(ROWS, 128), shape_of(24, 128),
        ],
        [pltpu.VMEM((PAIRED, 128), F32)],
    )(phases.reshape(4, ROWS, CY), solutes.reshape(3, ROWS, CY), small, slab)
    even = lax.ppermute(even, "gz", [(0, 1), (1, 0), (2, 3), (3, 2)])
    odd = lax.ppermute(odd, "gz", [(1, 2), (2, 1)])
    above2_early, above2 = lax.cond(
        shift_rows[0] >= 7,
        lambda rows: tuple(shifted(part, "gz", -2, False) for part in rows),
        lambda rows: rows,
        (early, second),
    )
    meta, plain = lax.optimization_barrier((meta, plain))

    low, high = call(
        pack_x,
        [VMEM] * 6 + [SMEM],
        [shape_of(KEPT * X_ROWS + 4, 128)] * 2,
        [pltpu.VMEM((17 * STRIP, 128), F32)],
    )(strip, even, odd, above2_early, meta, plain.reshape(1, 11), slab)
    before = shifted(high, "gx", 1, True)
    after = shifted(low, "gx", -1, True)
    late_bulk, _ = lax.optimization_barrier((bulk, low))
    above = shifted(late_bulk, "gz", -1, False)
    turned, slots = call(
        turn_columns,
        [VMEM] * 6 + [SMEM] * 2,
        [shape_of(56, 128), jax.ShapeDtypeStruct((32,), jnp.int32)],
        [pltpu.VMEM((17 * CX, 128), F32), pltpu.VMEM((128, 128), F32), pltpu.SMEM((64,), jnp.int32)],
        out_specs=[VMEM, SMEM],
    )(columns, even, odd, above2_early, meta, plain.reshape(1, 11), slab, balance)

    face_up, face_down = call(
        pack_y, [VMEM] * 3, [shape_of(32, 128)] * 2, [pltpu.VMEM((128, 128), F32)]
    )(turned, before, after)
    left = shifted(face_up, "gy", 1, True)
    right = shifted(face_down, "gy", -1, True)

    phases_out, solutes_out, send = call(
        steps,
        [VMEM] * 11 + [SMEM] * 4,
        [shape_of(4, ROWS, CY), shape_of(3, ROWS, CY), shape_of(64, 48, 128)],
        [
            pltpu.VMEM((KEPT, 19 * CX, 128), F32),
            pltpu.VMEM((HELD, WINDOW * CX, 128), F32),
            pltpu.VMEM((128, 128), F32),
            pltpu.VMEM((128, 128), F32),
            pltpu.VMEM((HELD, 10 * CX, 128), F32),
            pltpu.VMEM((2 * HELD, 24, 128), F32),
            pltpu.VMEM((2 * HELD, 8, 128), F32),
            pltpu.VMEM((8 * ROWS, 128), F32),
        ],
    )(
        bulk, above, above2, even, odd, before, after, turned, left, right, meta, slots, slab, plain, table,
    )
    arrived = lax.all_to_all(send, ("gx", "gy"), split_axis=0, concat_axis=0, tiled=True)
    (moved,) = call(place, [VMEM], [shape_of(7, 32, 512)], [pltpu.SMEM((65,), jnp.int32)])(arrived)
    return (
        phases_out.reshape(4, CZ, CX, CY),
        solutes_out.reshape(3, CZ, CX, CY),
        jnp.transpose(moved, (1, 0, 2)),
    )


def solution(mesh):
    block = P(None, "gz", "gx", "gy")
    table = P("gz", "gx", "gy", None)
    return jax.shard_map(
        per_device,
        mesh=mesh,
        in_specs=(block, block, P(), P(), table, table, P(), P(), P(), P(), P(), P()),
        out_specs=(block, block, P(("gz", "gx", "gy"), None, None)),
        check_vma=False,
    )
```

```python
import jax
import jax.numpy as jnp
from jax import lax
from jax.experimental import pallas as pl
from jax.experimental.pallas import tpu as pltpu
from jax.sharding import PartitionSpec as P

CZ, CX, CY = 8, 16, 128
KEPT = 6
HELD = KEPT + 3
WINDOW = CZ + 4
ROWS = CZ * CX
X_ROWS = 18
MARKER = 3.0e38
LIMIT = 1.0e30
F32 = jnp.float32

VMEM = pl.BlockSpec(memory_space=pltpu.VMEM)
SMEM = pl.BlockSpec(memory_space=pltpu.SMEM)


def lanes_of(rows):
    return lax.broadcasted_iota(jnp.int32, (rows, 128), 1)


def sublanes_of(rows):
    return lax.broadcasted_iota(jnp.int32, (rows, 128), 0)


def flag_row(small_ref, b):
    group = lanes_of(8) // 8
    row = jnp.zeros((8, 128), F32)
    for d in range(16):
        row = jnp.where(group == d, small_ref[b * 16 + d].astype(F32), row)
    return row


LAYERS = (0, 1, 14, 15)
STRIP = 24
PAIRED = 8 * STRIP + 32


def gather(rows, value_of):
    lane = lanes_of(rows)
    packed = jnp.zeros((rows, 128), F32)
    for c in range(KEPT):
        moved = pltpu.roll(value_of(c), 2 + 4 * c, 1)
        packed = jnp.where((lane >= 4 * c) & (lane < 4 * c + 4), moved, packed)
    return packed


def pack_z(
    phases_ref, solutes_ref, small_ref, slab_ref,
    bulk_ref, second_ref, even_ref, odd_ref, strip_ref, columns_ref, meta_ref,
    last_ref,
):
    flags = jnp.concatenate([flag_row(small_ref, b) for b in range(2)], axis=0)
    bulk_ref[KEPT * ROWS : KEPT * ROWS + CX] = flags
    last_ref[KEPT * CX : (KEPT + 1) * CX] = flags
    meta_ref[0:8] = jnp.full((8, 128), small_ref[32].astype(F32), F32)
    meta_ref[8:24] = flags
    for c in range(KEPT):
        source = phases_ref.at[c] if c < 3 else solutes_ref.at[c - 3]
        bulk_ref[c * ROWS : (c + 1) * ROWS] = source[...]
        second_ref[2 * c * CX : 2 * (c + 1) * CX] = bulk_ref[c * ROWS : c * ROWS + 2 * CX]
        last_ref[c * CX : (c + 1) * CX] = bulk_ref[c * ROWS + 7 * CX : (c + 1) * ROWS]
        for n, x in enumerate(LAYERS):
            strip_ref[pl.ds(n * KEPT + c, 8, stride=STRIP)] = bulk_ref[pl.ds(c * ROWS + x, 8, stride=CX)]
    flags = pltpu.roll(flags, 25, 1)
    flag_lane = (lanes_of(CX) == 24) | (lanes_of(CX) == 25)
    for z in range(CZ):
        packed = gather(CX, lambda c: bulk_ref[c * ROWS + z * CX : c * ROWS + (z + 1) * CX])
        columns_ref[z * CX : (z + 1) * CX] = jnp.where(flag_lane, flags, packed)
    strip_ref[8 * STRIP : PAIRED] = columns_ref[...].T[0:32]
    is_even = (slab_ref[0] & 1) == 0
    last_ref[(KEPT + 1) * CX : PAIRED] = jnp.zeros((PAIRED - (KEPT + 1) * CX, 128), F32)
    even_ref[...] = jnp.where(is_even, last_ref[...], strip_ref[...])
    odd_ref[...] = jnp.where(is_even, strip_ref[...], last_ref[...])


def melt_of(row_ref, k):
    row = row_ref[...]
    lane = lax.broadcasted_iota(jnp.int32, row.shape, 1)
    return jnp.sum(jnp.where(lane == k, row, 0.0), axis=1, keepdims=True)


def window_ends(meta_ref, slab_ref):
    shift = jnp.max(meta_ref[0:1]).astype(jnp.int32)
    slab = slab_ref[0]
    return shift, jnp.where(slab == 0, shift, shift - 1), jnp.where(slab == 3, shift + 7, shift + 8)


def pack_x(own_ref, even_ref, odd_ref, above2_ref, meta_ref, row_ref, slab_ref, low_ref, high_ref, raw_ref):
    slab = slab_ref[0]
    shift, first, last = window_ends(meta_ref, slab_ref)
    fresh = jnp.zeros((STRIP, 128), F32)
    sub = sublanes_of(STRIP) % KEPT
    for k in range(3):
        fresh = jnp.where(sub == 3 + k, melt_of(row_ref, k), fresh)
    raw_ref[0 : 8 * STRIP] = own_ref[0 : 8 * STRIP]
    for z in range(CZ):
        rows = slice(z * STRIP, (z + 1) * STRIP)
        here = jnp.where((slab & 1) == 0, even_ref[rows], odd_ref[rows])
        raw_ref[(8 + z) * STRIP : (9 + z) * STRIP] = jnp.where(slab == 3, fresh, here)
    for n, x in enumerate(LAYERS):
        raw_ref[16 * STRIP + n * KEPT : 16 * STRIP + (n + 1) * KEPT] = above2_ref[pl.ds(x, KEPT, stride=2 * CX)]

    @pl.when(slab >= 2)
    def _():
        raw_ref[16 * STRIP : 17 * STRIP] = fresh

    for i in range(10):
        row = first if i == 0 else last if i == 9 else shift + (i - 1)
        value = raw_ref[pl.ds(pl.multiple_of(row * STRIP, 8), STRIP)]
        low_ref[pl.ds(i, KEPT, stride=X_ROWS)] = value[0:6]
        high_ref[pl.ds(i, KEPT, stride=X_ROWS)] = value[18:24]
        if 0 < i < 9:
            low_ref[pl.ds(9 + i, KEPT, stride=X_ROWS)] = value[6:12]
            high_ref[pl.ds(9 + i, KEPT, stride=X_ROWS)] = value[12:18]
    flags = meta_ref[8:24]
    low_ref[KEPT * X_ROWS : KEPT * X_ROWS + 4] = flags[0:4]
    high_ref[KEPT * X_ROWS : KEPT * X_ROWS + 4] = flags[12:16]


def turn_columns(
    columns_ref, even_ref, odd_ref, above2_ref, meta_ref, row_ref, slab_ref, balance_ref,
    out_ref, slots_ref, raw_ref, wide_ref, given_ref,
):
    for owner in range(64):
        given_ref[owner] = jnp.int32(0)
    for t in range(32):
        owner = balance_ref[0, 0, 0, t]
        slots_ref[t] = 2 * owner + given_ref[owner]
        given_ref[owner] = jnp.int32(1)

    slab = slab_ref[0]
    shift, first, last = window_ends(meta_ref, slab_ref)
    fresh = jnp.zeros((CX, 128), F32)
    part = lanes_of(CX) // 4
    for k in range(3):
        fresh = jnp.where(part == 3 + k, melt_of(row_ref, k), fresh)
    raw_ref[0:ROWS] = columns_ref[...]
    wide_ref[...] = jnp.zeros((128, 128), F32)
    wide_ref[0:32] = jnp.where((slab & 1) == 0, even_ref[8 * STRIP : PAIRED], odd_ref[8 * STRIP : PAIRED])
    raw_ref[ROWS : 2 * ROWS] = wide_ref[...].T

    @pl.when(slab == 3)
    def _():
        for z in range(CZ):
            raw_ref[ROWS + z * CX : ROWS + (z + 1) * CX] = fresh

    raw_ref[2 * ROWS : 2 * ROWS + CX] = jnp.where(
        slab >= 2, fresh, gather(CX, lambda c: above2_ref[2 * c * CX : (2 * c + 1) * CX])
    )

    def rows_at(row):
        return raw_ref[pl.ds(pl.multiple_of(row * CX, CX), CX)]

    flag_lane = (lanes_of(CX) == 24) | (lanes_of(CX) == 25)
    for z in range(CZ):
        wide_ref[z * CX : (z + 1) * CX] = jnp.where(flag_lane, columns_ref[0:CX], rows_at(shift + z))
    out_ref[0:32] = wide_ref[...].T[0:32]
    wide_ref[...] = jnp.zeros((128, 128), F32)
    wide_ref[0:CX] = rows_at(first)
    wide_ref[112:128] = rows_at(last)
    out_ref[32:56] = wide_ref[...].T[0:24]


def pack_y(turned_ref, before_ref, after_ref, up_ref, down_ref, sides_ref):
    sides_ref[...] = jnp.zeros((128, 128), F32)
    sides_ref[pl.ds(0, 8, stride=CX)] = gather(8, lambda c: before_ref[c * X_ROWS + 1 : c * X_ROWS + 9])
    sides_ref[pl.ds(15, 8, stride=CX)] = gather(8, lambda c: after_ref[c * X_ROWS + 1 : c * X_ROWS + 9])
    sides_ref[...] = sides_ref[...].T
    for ref, near, far in ((up_ref, 1, 0), (down_ref, 2, 3)):
        ref[0:6] = turned_ref[pl.ds(near, KEPT, stride=4)]
        ref[6:12] = turned_ref[pl.ds(far, KEPT, stride=4)]
        ref[12:18] = turned_ref[pl.ds(32 + near, KEPT, stride=4)]
        ref[18:24] = sides_ref[pl.ds(near, KEPT, stride=4)]
        ref[24:25] = turned_ref[23 + near : 24 + near]


def read_parameters(table_ref, plain_ref):
    stiffness = [[table_ref[a, e] for e in range(3)] for a in range(4)]
    return dict(
        stiffness=stiffness,
        total=[row[0] + row[1] + row[2] for row in stiffness],
        coupling=[[table_ref[a, 3 + k] for k in range(3)] for a in range(4)],
        base=[0.5 * table_ref[3, 6 + k] for k in range(3)],
        excess=[[0.5 * (table_ref[a, 6 + k] - table_ref[3, 6 + k]) for k in range(3)] for a in range(3)],
        release=[[table_ref[a, 9 + k] for k in range(3)] for a in range(4)],
        barrier=[plain_ref[3 + a] for a in range(4)],
        twice=[2.0 * plain_ref[3 + a] for a in range(4)],
        slope=[plain_ref[7 + a] for a in range(4)],
    )


def with_densities(kept_values, par):
    p = kept_values[:3]
    return list(kept_values) + [
        par["base"][k] + (par["excess"][0][k] * p[0] + par["excess"][1][k] * p[1] + par["excess"][2][k] * p[2])
        for k in range(3)
    ]


def flows(own, beside):
    return [(own[6 + k] + beside[6 + k]) * (beside[3 + k] - own[3 + k]) for k in range(3)]


def advance(own, neighbours, flag, height, par, flow_below=None):
    others = own[0] + own[1] + own[2]
    fractions = [own[0], own[1], own[2], 1.0 - others]
    solutes = own[3:6]
    stiffness = par["stiffness"]
    total = par["total"]
    laplace = [(-2.0 * total[a]) * own[a] for a in range(3)] + [(2.0 * total[3]) * others]
    gains = None
    flow_above = None
    for e, (upper, lower) in enumerate(neighbours):
        sums = [upper[a] + lower[a] for a in range(3)]
        for a in range(3):
            laplace[a] = laplace[a] + stiffness[a][e] * sums[a]
        laplace[3] = laplace[3] - stiffness[3][e] * (sums[0] + sums[1] + sums[2])
        gained = flows(own, upper)
        if e == 0:
            flow_above = gained
        if e == 0 and flow_below is not None:
            gained = [gained[k] - flow_below[k] for k in range(3)]
        else:
            more = flows(own, lower)
            gained = [gained[k] + more[k] for k in range(3)]
        gains = gained if e == 0 else [gains[k] + gained[k] for k in range(3)]
    rates = []
    for a in range(4):
        p = fractions[a]
        drive = (par["slope"][a] * height - par["barrier"][a]) + par["twice"][a] * p
        for k in range(3):
            drive = drive + par["coupling"][a][k] * solutes[k]
        rates.append(flag * (laplace[a] + (p - p * p) * drive))
    mean = 0.25 * ((rates[0] + rates[1]) + (rates[2] + rates[3]))
    changes = [rate - mean for rate in rates]
    after = [fractions[a] + changes[a] for a in range(4)]
    for k in range(3):
        released = par["release"][0][k] * changes[0]
        for a in range(1, 4):
            released = released + par["release"][a][k] * changes[a]
        after.append(solutes[k] + (gains[k] + released))
    return after[:3] + after[4:], after[3], flow_above


def steps(
    own_ref, above_ref, above2_ref, even_ref, odd_ref, before_ref, after_ref, own_y_ref, left_ref, right_ref, meta_ref,
    slots_ref, slab_ref, plain_ref, table_ref,
    phases_ref, solutes_ref, send_ref,
    raw_ref, window_ref, edge_ref, turned_ref, first_ref, side_ref, xface_ref, final_ref,
):
    slab = slab_ref[0]
    at_bottom = slab == 0
    at_top = slab == 3
    par = read_parameters(table_ref, plain_ref)
    first_row = (slab * CZ).astype(F32)

    def height_of(z):
        return (first_row + z + 0.5) / 32.0 - 0.5

    lane16, lane8, sub16 = lanes_of(CX), lanes_of(8), sublanes_of(CX)
    flags = own_ref[KEPT * ROWS : KEPT * ROWS + CX]

    def below(c):
        rows = slice(c * CX, (c + 1) * CX)
        return jnp.where((slab & 1) == 0, odd_ref[rows], even_ref[rows])

    shift = jnp.max(meta_ref[0:1]).astype(jnp.int32)
    for c in range(KEPT):
        fresh = jnp.full((CX, 128), plain_ref[c - 3] if c >= 3 else 0.0, F32)
        raw_ref[c, 0:CX] = below(c)
        raw_ref[c, CX : 9 * CX] = own_ref[c * ROWS : (c + 1) * ROWS]
        for z in range(CZ):
            here = above_ref[c * ROWS + z * CX : c * ROWS + (z + 1) * CX]
            raw_ref[c, (9 + z) * CX : (10 + z) * CX] = jnp.where(at_top, fresh, here)
        for z in range(2):
            here = above2_ref[(2 * c + z) * CX : (2 * c + z + 1) * CX]
            raw_ref[c, (17 + z) * CX : (18 + z) * CX] = jnp.where(slab >= 2, fresh, here)
        for w in range(WINDOW):
            row = shift - 1 + w
            if w == 1:
                row = jnp.where(at_bottom, row + 1, row)
            if w == WINDOW - 2:
                row = jnp.where(at_top, row - 1, row)
            window_ref[c, w * CX : (w + 1) * CX] = raw_ref[c, pl.ds(pl.multiple_of(row * CX, CX), CX)]

    for w in range(WINDOW):
        rows = slice(w * CX, (w + 1) * CX)
        held = with_densities([window_ref[c, rows] for c in range(KEPT)], par)
        for c in range(KEPT, HELD):
            window_ref[c, rows] = held[c]
    for side, ref in ((0, before_ref), (1, after_ref)):
        held = with_densities([ref[c * X_ROWS : (c + 1) * X_ROWS] for c in range(KEPT)], par)
        for c in range(HELD):
            side_ref[side * HELD + c, 0:X_ROWS] = held[c]

    edge_ref[...] = jnp.zeros((128, 128), F32)
    for group, start in ((0, 0), (1, 12), (2, 18)):
        for ref, odd_row in ((right_ref, 0), (left_ref, 1)):
            held = with_densities([ref[start + c : start + c + 1] for c in range(KEPT)], par)
            for c in range(HELD):
                at = group * 2 * HELD + 2 * c + odd_row
                edge_ref[at : at + 1] = held[c]
    turned_ref[...] = edge_ref[...].T

    def beside_y(value, rows, column):
        lane = lane16 if value.shape[0] == CX else lane8
        fill = pltpu.roll(rows, 127 - column, 1)
        upper = jnp.where(lane == 127, fill, pltpu.roll(value, 127, 1))
        lower = jnp.where(lane == 0, fill, pltpu.roll(value, 1, 1))
        return upper, lower

    def beside_x(ref, c, start, low_row, high_row):
        upper = jnp.where(sub16 == 15, high_row, ref[c, start + 1 : start + 1 + CX])
        lower = jnp.where(sub16 == 0, low_row, ref[c, start - 1 : start - 1 + CX])
        return upper, lower

    def split(pairs):
        return ([pair[0] for pair in pairs], [pair[1] for pair in pairs])

    def store_held(ref, rows, values):
        for c, value in enumerate(with_densities(values, par)):
            ref[c, rows] = value

    flow = None
    for w in range(1, WINDOW - 1):
        z = w - 2
        start = w * CX
        own = [window_ref[c, start : start + CX] for c in range(HELD)]
        along_z = (
            [window_ref[c, start + CX : start + 2 * CX] for c in range(HELD)],
            [window_ref[c, start - CX : start] for c in range(HELD)],
        )
        along_x = split(
            [
                beside_x(
                    window_ref, c, start,
                    side_ref[c, z + 1 : z + 2], side_ref[HELD + c, z + 1 : z + 2],
                )
                for c in range(HELD)
            ]
        )
        if z == -1:
            rows, group, flag = turned_ref[0:CX], 1, below(KEPT)
        elif z == CZ:
            rows, group, flag = turned_ref[112:128], 1, above_ref[KEPT * ROWS : KEPT * ROWS + CX]
        else:
            rows, group, flag = turned_ref[z * CX : (z + 1) * CX], 0, flags
        along_y = split([beside_y(own[c], rows, 2 * (group * HELD + c)) for c in range(HELD)])
        result, _, flow = advance(own, (along_z, along_x, along_y), flag, height_of(z), par, flow)
        store_held(first_ref, slice((w - 1) * CX, w * CX), result)

    @pl.when(at_bottom)
    def _():
        for c in range(HELD):
            first_ref[c, 0:CX] = first_ref[c, CX : 2 * CX]

    @pl.when(at_top)
    def _():
        for c in range(HELD):
            first_ref[c, 9 * CX : 10 * CX] = first_ref[c, 8 * CX : 9 * CX]

    face_height = height_of(sublanes_of(8).astype(F32))
    for side, ref, x in ((0, before_ref, 0), (1, after_ref, 15)):
        layers = [side_ref.at[side * HELD + c] for c in range(HELD)]
        own = [layer[1:9] for layer in layers]
        along_z = ([layer[2:10] for layer in layers], [layer[0:8] for layer in layers])
        along_x = (
            [layer[10:18] for layer in layers],
            [window_ref[c, pl.ds(2 * CX + x, 8, stride=CX)] for c in range(HELD)],
        )
        rows = turned_ref[pl.ds(x, 8, stride=CX)]
        along_y = split([beside_y(own[c], rows, 2 * (2 * HELD + c)) for c in range(HELD)])
        at = KEPT * X_ROWS + (3 if side == 0 else 0)
        flag = ref[at : at + 1]
        result, _, _ = advance(own, (along_z, along_x, along_y), flag, face_height, par)
        for c, value in enumerate(with_densities(result, par)):
            xface_ref[side * HELD + c] = value

    sub8 = sublanes_of(8)

    def both(right_row, left_row):
        return jnp.where(sub8 == 0, right_row, left_row)

    def lifted(c, start):
        return both(right_ref[start + c : start + c + 1], left_ref[start + c : start + c + 1])

    own, ends, sides, outer = [
        with_densities([lifted(c, start) for c in range(KEPT)], par) for start in (0, 12, 18, 6)
    ]
    inner = with_densities(
        [both(own_y_ref[4 * c + 1 : 4 * c + 2], own_y_ref[4 * c + 2 : 4 * c + 3]) for c in range(KEPT)], par
    )
    along_z = (
        [jnp.where(lane8 >= 112, ends[c], pltpu.roll(own[c], 112, 1)) for c in range(HELD)],
        [jnp.where(lane8 < 16, ends[c], pltpu.roll(own[c], 16, 1)) for c in range(HELD)],
    )
    along_x = (
        [jnp.where(lane8 % 16 == 15, sides[c], pltpu.roll(own[c], 127, 1)) for c in range(HELD)],
        [jnp.where(lane8 % 16 == 0, sides[c], pltpu.roll(own[c], 1, 1)) for c in range(HELD)],
    )
    flag = both(right_ref[24:25], left_ref[24:25])
    result, _, _ = advance(
        own, (along_z, along_x, (outer, inner)), flag, height_of((lane8 // 16).astype(F32)), par
    )
    for c, value in enumerate(with_densities(result, par)):
        edge_ref[2 * c : 2 * c + 2] = value[0:2]
    turned_ref[...] = edge_ref[...].T

    flow = None
    for z in range(CZ):
        start = (z + 1) * CX
        own = [first_ref[c, start : start + CX] for c in range(HELD)]
        along_z = (
            [first_ref[c, start + CX : start + 2 * CX] for c in range(HELD)],
            [first_ref[c, start - CX : start] for c in range(HELD)],
        )
        along_x = split(
            [
                beside_x(first_ref, c, start, xface_ref[c, z : z + 1], xface_ref[HELD + c, z : z + 1])
                for c in range(HELD)
            ]
        )
        rows = turned_ref[z * CX : (z + 1) * CX]
        along_y = split([beside_y(own[c], rows, 2 * c) for c in range(HELD)])
        result, last, flow = advance(own, (along_z, along_x, along_y), flags, height_of(z), par, flow)
        for c in range(3):
            phases_ref[c, z * CX : (z + 1) * CX] = result[c]
            solutes_ref[c, z * CX : (z + 1) * CX] = result[3 + c]
        phases_ref[3, z * CX : (z + 1) * CX] = last
        for c in range(KEPT):
            final_ref[c * ROWS + z * CX : c * ROWS + (z + 1) * CX] = result[c]

    for owner in range(64):
        send_ref[owner, 0:1] = jnp.full((1, 128), MARKER, F32)
    group = lane8 // 8
    for b in range(2):
        for q in range(4):
            parts = []
            for i in range(16):
                row = (2 * q + i // 8) * CX + b * 8 + i % 8
                parts.append(final_ref[pl.ds(row, 8, stride=ROWS)])
            for step in (8, 4, 2, 1):
                keep = (group & step) == 0
                swapped = list(parts)
                for i in range(16):
                    if i & step == 0:
                        one, two = parts[i], parts[i + step]
                        swapped[i] = jnp.where(keep, one, pltpu.roll(two, step * 8, 1))
                        swapped[i + step] = jnp.where(keep, pltpu.roll(one, 128 - step * 8, 1), two)
                parts = swapped
            for d in range(16):
                slot = slots_ref[b * 16 + d]
                send_ref[slot >> 1, pl.ds(2 * q + (slot & 1), KEPT, stride=8)] = parts[d][0:6]


def place(arrived_ref, moved_ref, sources):
    sub16 = sublanes_of(16)
    weight = jnp.zeros((16, 128), F32)
    for i in range(16):
        weight = jnp.where((sub16 == i) & (lanes_of(16) == 0), float(2**i), weight)
    masks = []
    for block in range(4):
        first = jnp.concatenate([arrived_ref[block * 16 + i, 0:1] for i in range(16)], axis=0)
        masks.append(jnp.sum(jnp.where(first < LIMIT, weight, 0.0)).astype(jnp.int32))
    count = jnp.int32(0)
    for source in range(64):
        sources[count] = source
        count = count + ((masks[source // 16] >> (source % 16)) & 1)
    for n in range(0, 16, 4):
        group = [sources[n + i] & 63 for i in range(4)]
        rows = slice(2 * n, 2 * n + 8)
        for q in range(4):
            span = slice(q * 128, (q + 1) * 128)
            parts = []
            for c in range(KEPT):
                at = 8 * c + 2 * q
                parts.append(jnp.concatenate([arrived_ref[s, at : at + 2] for s in group], axis=0))
            for c in range(3):
                moved_ref[c, rows, span] = parts[c]
                moved_ref[4 + c, rows, span] = parts[3 + c]
            moved_ref[3, rows, span] = 1.0 - (parts[0] + parts[1] + parts[2])


def shape_of(*dims):
    return jax.ShapeDtypeStruct(dims, F32)


PARAMS = pltpu.CompilerParams(vmem_limit_bytes=32 * 1024 * 1024)


def call(body, ins, outs, scratch=(), out_specs=None):
    return pl.pallas_call(
        body,
        in_specs=list(ins),
        out_specs=out_specs or [VMEM] * len(outs),
        out_shape=list(outs),
        scratch_shapes=list(scratch),
        compiler_params=PARAMS,
        cost_estimate=pl.CostEstimate(flops=0, bytes_accessed=1000000, transcendentals=0),
    )


def shifted(value, axis, by, wrap):
    count = lax.axis_size(axis)
    pairs = [
        (source, (source + by) % count) for source in range(count) if wrap or 0 <= source + by < count
    ]
    return lax.ppermute(value, axis, pairs)


def per_device(
    phases, solutes, melt, shift_rows, flags, balance,
    stiffness, barrier, coupling, slope, diffusivity, release,
):
    slab = lax.axis_index("gz").astype(jnp.int32).reshape(1)
    small = jnp.concatenate([flags.reshape(32), shift_rows])
    plain = jnp.concatenate([melt, barrier, slope])
    table = jnp.concatenate([stiffness, coupling, diffusivity, release], axis=1)
    bulk, second, even, odd, strip, columns, meta = call(
        pack_z,
        [VMEM] * 2 + [SMEM] * 2,
        [
            shape_of(KEPT * ROWS + CX, 128), shape_of(KEPT * 2 * CX, 128),
            shape_of(PAIRED, 128), shape_of(PAIRED, 128), shape_of(PAIRED, 128), shape_of(ROWS, 128), shape_of(24, 128),
        ],
        [pltpu.VMEM((PAIRED, 128), F32)],
    )(phases.reshape(4, ROWS, CY), solutes.reshape(3, ROWS, CY), small, slab)
    even = lax.ppermute(even, "gz", [(0, 1), (1, 0), (2, 3), (3, 2)])
    odd = lax.ppermute(odd, "gz", [(1, 2), (2, 1)])
    above2 = lax.cond(
        shift_rows[0] >= 7, lambda rows: shifted(rows, "gz", -2, False), lambda rows: rows, second
    )
    meta, plain = lax.optimization_barrier((meta, plain))

    low, high = call(
        pack_x,
        [VMEM] * 6 + [SMEM],
        [shape_of(KEPT * X_ROWS + 4, 128)] * 2,
        [pltpu.VMEM((17 * STRIP, 128), F32)],
    )(strip, even, odd, above2, meta, plain.reshape(1, 11), slab)
    before = shifted(high, "gx", 1, True)
    after = shifted(low, "gx", -1, True)
    late_bulk, _ = lax.optimization_barrier((bulk, low))
    above = shifted(late_bulk, "gz", -1, False)
    turned, slots = call(
        turn_columns,
        [VMEM] * 6 + [SMEM] * 2,
        [shape_of(56, 128), jax.ShapeDtypeStruct((32,), jnp.int32)],
        [pltpu.VMEM((17 * CX, 128), F32), pltpu.VMEM((128, 128), F32), pltpu.SMEM((64,), jnp.int32)],
        out_specs=[VMEM, SMEM],
    )(columns, even, odd, above2, meta, plain.reshape(1, 11), slab, balance)

    face_up, face_down = call(
        pack_y, [VMEM] * 3, [shape_of(32, 128)] * 2, [pltpu.VMEM((128, 128), F32)]
    )(turned, before, after)
    left = shifted(face_up, "gy", 1, True)
    right = shifted(face_down, "gy", -1, True)

    phases_out, solutes_out, send = call(
        steps,
        [VMEM] * 11 + [SMEM] * 4,
        [shape_of(4, ROWS, CY), shape_of(3, ROWS, CY), shape_of(64, 48, 128)],
        [
            pltpu.VMEM((KEPT, 19 * CX, 128), F32),
            pltpu.VMEM((HELD, WINDOW * CX, 128), F32),
            pltpu.VMEM((128, 128), F32),
            pltpu.VMEM((128, 128), F32),
            pltpu.VMEM((HELD, 10 * CX, 128), F32),
            pltpu.VMEM((2 * HELD, 24, 128), F32),
            pltpu.VMEM((2 * HELD, 8, 128), F32),
            pltpu.VMEM((8 * ROWS, 128), F32),
        ],
    )(
        bulk, above, above2, even, odd, before, after, turned, left, right, meta, slots, slab, plain, table,
    )
    arrived = lax.all_to_all(send, ("gx", "gy"), split_axis=0, concat_axis=0, tiled=True)
    (moved,) = call(place, [VMEM], [shape_of(7, 32, 512)], [pltpu.SMEM((65,), jnp.int32)])(arrived)
    return (
        phases_out.reshape(4, CZ, CX, CY),
        solutes_out.reshape(3, CZ, CX, CY),
        jnp.transpose(moved, (1, 0, 2)),
    )


def solution(mesh):
    block = P(None, "gz", "gx", "gy")
    table = P("gz", "gx", "gy", None)
    return jax.shard_map(
        per_device,
        mesh=mesh,
        in_specs=(block, block, P(), P(), table, table, P(), P(), P(), P(), P(), P()),
        out_specs=(block, block, P(("gz", "gx", "gy"), None, None)),
        check_vma=False,
    )
```

```python
import functools

import jax
import jax.numpy as jnp
from jax import lax
from jax.experimental import pallas as pl
from jax.experimental.pallas import tpu as pltpu
from jax.sharding import PartitionSpec as P

CZ, CX, CY = 8, 16, 128
KEPT = 6
HELD = KEPT + 3
WINDOW = CZ + 4
ROWS = CZ * CX
X_ROWS = 18
MARKER = 3.0e38
LIMIT = 1.0e30
F32 = jnp.float32

VMEM = pl.BlockSpec(memory_space=pltpu.VMEM)
SMEM = pl.BlockSpec(memory_space=pltpu.SMEM)


def lanes_of(rows):
    return lax.broadcasted_iota(jnp.int32, (rows, 128), 1)


def sublanes_of(rows):
    return lax.broadcasted_iota(jnp.int32, (rows, 128), 0)


def flag_row(small_ref, b):
    group = lanes_of(8) // 8
    row = jnp.zeros((8, 128), F32)
    for d in range(16):
        row = jnp.where(group == d, small_ref[b * 16 + d].astype(F32), row)
    return row


LAYERS = (0, 1, 14, 15)
STRIP = 24
PAIRED = 8 * STRIP + 32


def gather(rows, value_of):
    lane = lanes_of(rows)
    packed = jnp.zeros((rows, 128), F32)
    for c in range(KEPT):
        moved = pltpu.roll(value_of(c), 2 + 4 * c, 1)
        packed = jnp.where((lane >= 4 * c) & (lane < 4 * c + 4), moved, packed)
    return packed


def pack_z(
    phases_ref, solutes_ref, small_ref, slab_ref,
    bulk_ref, second_ref, even_ref, odd_ref, strip_ref, columns_ref, meta_ref,
    last_ref,
):
    flags = jnp.concatenate([flag_row(small_ref, b) for b in range(2)], axis=0)
    bulk_ref[KEPT * ROWS : KEPT * ROWS + CX] = flags
    last_ref[KEPT * CX : (KEPT + 1) * CX] = flags
    meta_ref[0:8] = jnp.full((8, 128), small_ref[32].astype(F32), F32)
    meta_ref[8:24] = flags
    for c in range(KEPT):
        source = phases_ref.at[c] if c < 3 else solutes_ref.at[c - 3]
        bulk_ref[c * ROWS : (c + 1) * ROWS] = source[...]
        second_ref[2 * c * CX : 2 * (c + 1) * CX] = bulk_ref[c * ROWS : c * ROWS + 2 * CX]
        last_ref[c * CX : (c + 1) * CX] = bulk_ref[c * ROWS + 7 * CX : (c + 1) * ROWS]
        for n, x in enumerate(LAYERS):
            strip_ref[pl.ds(n * KEPT + c, 8, stride=STRIP)] = bulk_ref[pl.ds(c * ROWS + x, 8, stride=CX)]
    flags = pltpu.roll(flags, 25, 1)
    flag_lane = (lanes_of(CX) == 24) | (lanes_of(CX) == 25)
    for z in range(CZ):
        packed = gather(CX, lambda c: bulk_ref[c * ROWS + z * CX : c * ROWS + (z + 1) * CX])
        columns_ref[z * CX : (z + 1) * CX] = jnp.where(flag_lane, flags, packed)
    strip_ref[8 * STRIP : PAIRED] = columns_ref[...].T[0:32]
    is_even = (slab_ref[0] & 1) == 0
    last_ref[(KEPT + 1) * CX : PAIRED] = jnp.zeros((PAIRED - (KEPT + 1) * CX, 128), F32)
    even_ref[...] = jnp.where(is_even, last_ref[...], strip_ref[...])
    odd_ref[...] = jnp.where(is_even, strip_ref[...], last_ref[...])


def melt_of(row_ref, k):
    row = row_ref[...]
    lane = lax.broadcasted_iota(jnp.int32, row.shape, 1)
    return jnp.sum(jnp.where(lane == k, row, 0.0), axis=1, keepdims=True)


def window_ends(meta_ref, slab_ref):
    shift = jnp.max(meta_ref[0:1]).astype(jnp.int32)
    slab = slab_ref[0]
    return shift, jnp.where(slab == 0, shift, shift - 1), jnp.where(slab == 3, shift + 7, shift + 8)


def pack_x(own_ref, even_ref, odd_ref, above2_ref, meta_ref, row_ref, slab_ref, low_ref, high_ref, raw_ref):
    slab = slab_ref[0]
    shift, first, last = window_ends(meta_ref, slab_ref)
    fresh = jnp.zeros((STRIP, 128), F32)
    sub = sublanes_of(STRIP) % KEPT
    for k in range(3):
        fresh = jnp.where(sub == 3 + k, melt_of(row_ref, k), fresh)
    raw_ref[0 : 8 * STRIP] = own_ref[0 : 8 * STRIP]
    for z in range(CZ):
        rows = slice(z * STRIP, (z + 1) * STRIP)
        here = jnp.where((slab & 1) == 0, even_ref[rows], odd_ref[rows])
        raw_ref[(8 + z) * STRIP : (9 + z) * STRIP] = jnp.where(slab == 3, fresh, here)
    for n, x in enumerate(LAYERS):
        raw_ref[16 * STRIP + n * KEPT : 16 * STRIP + (n + 1) * KEPT] = above2_ref[pl.ds(x, KEPT, stride=2 * CX)]

    @pl.when(slab >= 2)
    def _():
        raw_ref[16 * STRIP : 17 * STRIP] = fresh

    for i in range(10):
        row = first if i == 0 else last if i == 9 else shift + (i - 1)
        value = raw_ref[pl.ds(pl.multiple_of(row * STRIP, 8), STRIP)]
        low_ref[pl.ds(i, KEPT, stride=X_ROWS)] = value[0:6]
        high_ref[pl.ds(i, KEPT, stride=X_ROWS)] = value[18:24]
        if 0 < i < 9:
            low_ref[pl.ds(9 + i, KEPT, stride=X_ROWS)] = value[6:12]
            high_ref[pl.ds(9 + i, KEPT, stride=X_ROWS)] = value[12:18]
    flags = meta_ref[8:24]
    low_ref[KEPT * X_ROWS : KEPT * X_ROWS + 4] = flags[0:4]
    high_ref[KEPT * X_ROWS : KEPT * X_ROWS + 4] = flags[12:16]


def turn_columns(
    columns_ref, even_ref, odd_ref, above2_ref, meta_ref, row_ref, slab_ref, balance_ref,
    out_ref, slots_ref, raw_ref, wide_ref, given_ref,
):
    for owner in range(64):
        given_ref[owner] = jnp.int32(0)
    for t in range(32):
        owner = balance_ref[0, 0, 0, t]
        slots_ref[t] = 2 * owner + given_ref[owner]
        given_ref[owner] = jnp.int32(1)

    slab = slab_ref[0]
    shift, first, last = window_ends(meta_ref, slab_ref)
    fresh = jnp.zeros((CX, 128), F32)
    part = lanes_of(CX) // 4
    for k in range(3):
        fresh = jnp.where(part == 3 + k, melt_of(row_ref, k), fresh)
    raw_ref[0:ROWS] = columns_ref[...]
    wide_ref[...] = jnp.zeros((128, 128), F32)
    wide_ref[0:32] = jnp.where((slab & 1) == 0, even_ref[8 * STRIP : PAIRED], odd_ref[8 * STRIP : PAIRED])
    raw_ref[ROWS : 2 * ROWS] = wide_ref[...].T

    @pl.when(slab == 3)
    def _():
        for z in range(CZ):
            raw_ref[ROWS + z * CX : ROWS + (z + 1) * CX] = fresh

    raw_ref[2 * ROWS : 2 * ROWS + CX] = jnp.where(
        slab >= 2, fresh, gather(CX, lambda c: above2_ref[2 * c * CX : (2 * c + 1) * CX])
    )

    def rows_at(row):
        return raw_ref[pl.ds(pl.multiple_of(row * CX, CX), CX)]

    flag_lane = (lanes_of(CX) == 24) | (lanes_of(CX) == 25)
    for z in range(CZ):
        wide_ref[z * CX : (z + 1) * CX] = jnp.where(flag_lane, columns_ref[0:CX], rows_at(shift + z))
    out_ref[0:32] = wide_ref[...].T[0:32]
    wide_ref[...] = jnp.zeros((128, 128), F32)
    wide_ref[0:CX] = rows_at(first)
    wide_ref[112:128] = rows_at(last)
    out_ref[32:56] = wide_ref[...].T[0:24]


def pack_y(turned_ref, before_ref, after_ref, up_ref, down_ref, sides_ref):
    sides_ref[...] = jnp.zeros((128, 128), F32)
    sides_ref[pl.ds(0, 8, stride=CX)] = gather(8, lambda c: before_ref[c * X_ROWS + 1 : c * X_ROWS + 9])
    sides_ref[pl.ds(15, 8, stride=CX)] = gather(8, lambda c: after_ref[c * X_ROWS + 1 : c * X_ROWS + 9])
    sides_ref[...] = sides_ref[...].T
    for ref, near, far in ((up_ref, 1, 0), (down_ref, 2, 3)):
        ref[0:6] = turned_ref[pl.ds(near, KEPT, stride=4)]
        ref[6:12] = turned_ref[pl.ds(far, KEPT, stride=4)]
        ref[12:18] = turned_ref[pl.ds(32 + near, KEPT, stride=4)]
        ref[18:24] = sides_ref[pl.ds(near, KEPT, stride=4)]
        ref[24:25] = turned_ref[23 + near : 24 + near]


def read_parameters(table_ref, plain_ref):
    stiffness = [[table_ref[a, e] for e in range(3)] for a in range(4)]
    return dict(
        stiffness=stiffness,
        total=[row[0] + row[1] + row[2] for row in stiffness],
        coupling=[[table_ref[a, 3 + k] for k in range(3)] for a in range(4)],
        base=[0.5 * table_ref[3, 6 + k] for k in range(3)],
        excess=[[0.5 * (table_ref[a, 6 + k] - table_ref[3, 6 + k]) for k in range(3)] for a in range(3)],
        release=[[table_ref[a, 9 + k] for k in range(3)] for a in range(4)],
        barrier=[plain_ref[3 + a] for a in range(4)],
        twice=[2.0 * plain_ref[3 + a] for a in range(4)],
        slope=[plain_ref[7 + a] for a in range(4)],
    )


def with_densities(kept_values, par):
    p = kept_values[:3]
    return list(kept_values) + [
        par["base"][k] + (par["excess"][0][k] * p[0] + par["excess"][1][k] * p[1] + par["excess"][2][k] * p[2])
        for k in range(3)
    ]


def flows(own, beside):
    return [(own[6 + k] + beside[6 + k]) * (beside[3 + k] - own[3 + k]) for k in range(3)]


def advance(own, neighbours, flag, height, par, flow_below=None):
    others = own[0] + own[1] + own[2]
    fractions = [own[0], own[1], own[2], 1.0 - others]
    solutes = own[3:6]
    stiffness = par["stiffness"]
    total = par["total"]
    laplace = [(-2.0 * total[a]) * own[a] for a in range(3)] + [(2.0 * total[3]) * others]
    gains = None
    flow_above = None
    for e, (upper, lower) in enumerate(neighbours):
        sums = [upper[a] + lower[a] for a in range(3)]
        for a in range(3):
            laplace[a] = laplace[a] + stiffness[a][e] * sums[a]
        laplace[3] = laplace[3] - stiffness[3][e] * (sums[0] + sums[1] + sums[2])
        gained = flows(own, upper)
        if e == 0:
            flow_above = gained
        if e == 0 and flow_below is not None:
            gained = [gained[k] - flow_below[k] for k in range(3)]
        else:
            more = flows(own, lower)
            gained = [gained[k] + more[k] for k in range(3)]
        gains = gained if e == 0 else [gains[k] + gained[k] for k in range(3)]
    rates = []
    for a in range(4):
        p = fractions[a]
        drive = (par["slope"][a] * height - par["barrier"][a]) + par["twice"][a] * p
        for k in range(3):
            drive = drive + par["coupling"][a][k] * solutes[k]
        rates.append(flag * (laplace[a] + (p - p * p) * drive))
    mean = 0.25 * ((rates[0] + rates[1]) + (rates[2] + rates[3]))
    changes = [rate - mean for rate in rates]
    after = [fractions[a] + changes[a] for a in range(4)]
    for k in range(3):
        released = par["release"][0][k] * changes[0]
        for a in range(1, 4):
            released = released + par["release"][a][k] * changes[a]
        after.append(solutes[k] + (gains[k] + released))
    return after[:3] + after[4:], after[3], flow_above


def steps(
    own_ref, above_ref, above2_ref, even_ref, odd_ref, before_ref, after_ref, own_y_ref, left_ref, right_ref, meta_ref,
    slots_ref, slab_ref, plain_ref, table_ref,
    phases_ref, solutes_ref, send_ref,
    raw_ref, window_ref, edge_ref, turned_ref, first_ref, side_ref, xface_ref, final_ref,
):
    slab = slab_ref[0]
    at_bottom = slab == 0
    at_top = slab == 3
    par = read_parameters(table_ref, plain_ref)
    first_row = (slab * CZ).astype(F32)

    def height_of(z):
        return (first_row + z + 0.5) / 32.0 - 0.5

    lane16, lane8, sub16 = lanes_of(CX), lanes_of(8), sublanes_of(CX)
    flags = own_ref[KEPT * ROWS : KEPT * ROWS + CX]

    def below(c):
        rows = slice(c * CX, (c + 1) * CX)
        return jnp.where((slab & 1) == 0, odd_ref[rows], even_ref[rows])

    shift = jnp.max(meta_ref[0:1]).astype(jnp.int32)
    for c in range(KEPT):
        fresh = jnp.full((CX, 128), plain_ref[c - 3] if c >= 3 else 0.0, F32)
        raw_ref[c, 0:CX] = below(c)
        raw_ref[c, CX : 9 * CX] = own_ref[c * ROWS : (c + 1) * ROWS]
        for z in range(CZ):
            here = above_ref[c * ROWS + z * CX : c * ROWS + (z + 1) * CX]
            raw_ref[c, (9 + z) * CX : (10 + z) * CX] = jnp.where(at_top, fresh, here)
        for z in range(2):
            here = above2_ref[(2 * c + z) * CX : (2 * c + z + 1) * CX]
            raw_ref[c, (17 + z) * CX : (18 + z) * CX] = jnp.where(slab >= 2, fresh, here)
        for w in range(WINDOW):
            row = shift - 1 + w
            if w == 1:
                row = jnp.where(at_bottom, row + 1, row)
            if w == WINDOW - 2:
                row = jnp.where(at_top, row - 1, row)
            window_ref[c, w * CX : (w + 1) * CX] = raw_ref[c, pl.ds(pl.multiple_of(row * CX, CX), CX)]

    for w in range(WINDOW):
        rows = slice(w * CX, (w + 1) * CX)
        held = with_densities([window_ref[c, rows] for c in range(KEPT)], par)
        for c in range(KEPT, HELD):
            window_ref[c, rows] = held[c]
    for side, ref in ((0, before_ref), (1, after_ref)):
        held = with_densities([ref[c * X_ROWS : (c + 1) * X_ROWS] for c in range(KEPT)], par)
        for c in range(HELD):
            side_ref[side * HELD + c, 0:X_ROWS] = held[c]

    edge_ref[...] = jnp.zeros((128, 128), F32)
    for group, start in ((0, 0), (1, 12), (2, 18)):
        for ref, odd_row in ((right_ref, 0), (left_ref, 1)):
            held = with_densities([ref[start + c : start + c + 1] for c in range(KEPT)], par)
            for c in range(HELD):
                at = group * 2 * HELD + 2 * c + odd_row
                edge_ref[at : at + 1] = held[c]
    turned_ref[...] = edge_ref[...].T

    def beside_y(value, rows, column):
        lane = lane16 if value.shape[0] == CX else lane8
        fill = pltpu.roll(rows, 127 - column, 1)
        upper = jnp.where(lane == 127, fill, pltpu.roll(value, 127, 1))
        lower = jnp.where(lane == 0, fill, pltpu.roll(value, 1, 1))
        return upper, lower

    def beside_x(ref, c, start, low_row, high_row):
        upper = jnp.where(sub16 == 15, high_row, ref[c, start + 1 : start + 1 + CX])
        lower = jnp.where(sub16 == 0, low_row, ref[c, start - 1 : start - 1 + CX])
        return upper, lower

    def split(pairs):
        return ([pair[0] for pair in pairs], [pair[1] for pair in pairs])

    def store_held(ref, rows, values):
        for c, value in enumerate(with_densities(values, par)):
            ref[c, rows] = value

    flow = None
    for w in range(1, WINDOW - 1):
        z = w - 2
        start = w * CX
        own = [window_ref[c, start : start + CX] for c in range(HELD)]
        along_z = (
            [window_ref[c, start + CX : start + 2 * CX] for c in range(HELD)],
            [window_ref[c, start - CX : start] for c in range(HELD)],
        )
        along_x = split(
            [
                beside_x(
                    window_ref, c, start,
                    side_ref[c, z + 1 : z + 2], side_ref[HELD + c, z + 1 : z + 2],
                )
                for c in range(HELD)
            ]
        )
        if z == -1:
            rows, group, flag = turned_ref[0:CX], 1, below(KEPT)
        elif z == CZ:
            rows, group, flag = turned_ref[112:128], 1, above_ref[KEPT * ROWS : KEPT * ROWS + CX]
        else:
            rows, group, flag = turned_ref[z * CX : (z + 1) * CX], 0, flags
        along_y = split([beside_y(own[c], rows, 2 * (group * HELD + c)) for c in range(HELD)])
        result, _, flow = advance(own, (along_z, along_x, along_y), flag, height_of(z), par, flow)
        store_held(first_ref, slice((w - 1) * CX, w * CX), result)

    @pl.when(at_bottom)
    def _():
        for c in range(HELD):
            first_ref[c, 0:CX] = first_ref[c, CX : 2 * CX]

    @pl.when(at_top)
    def _():
        for c in range(HELD):
            first_ref[c, 9 * CX : 10 * CX] = first_ref[c, 8 * CX : 9 * CX]

    face_height = height_of(sublanes_of(8).astype(F32))
    for side, ref, x in ((0, before_ref, 0), (1, after_ref, 15)):
        layers = [side_ref.at[side * HELD + c] for c in range(HELD)]
        own = [layer[1:9] for layer in layers]
        along_z = ([layer[2:10] for layer in layers], [layer[0:8] for layer in layers])
        along_x = (
            [layer[10:18] for layer in layers],
            [window_ref[c, pl.ds(2 * CX + x, 8, stride=CX)] for c in range(HELD)],
        )
        rows = turned_ref[pl.ds(x, 8, stride=CX)]
        along_y = split([beside_y(own[c], rows, 2 * (2 * HELD + c)) for c in range(HELD)])
        at = KEPT * X_ROWS + (3 if side == 0 else 0)
        flag = ref[at : at + 1]
        result, _, _ = advance(own, (along_z, along_x, along_y), flag, face_height, par)
        for c, value in enumerate(with_densities(result, par)):
            xface_ref[side * HELD + c] = value

    sub8 = sublanes_of(8)

    def both(right_row, left_row):
        return jnp.where(sub8 == 0, right_row, left_row)

    def lifted(c, start):
        return both(right_ref[start + c : start + c + 1], left_ref[start + c : start + c + 1])

    own, ends, sides, outer = [
        with_densities([lifted(c, start) for c in range(KEPT)], par) for start in (0, 12, 18, 6)
    ]
    inner = with_densities(
        [both(own_y_ref[4 * c + 1 : 4 * c + 2], own_y_ref[4 * c + 2 : 4 * c + 3]) for c in range(KEPT)], par
    )
    along_z = (
        [jnp.where(lane8 >= 112, ends[c], pltpu.roll(own[c], 112, 1)) for c in range(HELD)],
        [jnp.where(lane8 < 16, ends[c], pltpu.roll(own[c], 16, 1)) for c in range(HELD)],
    )
    along_x = (
        [jnp.where(lane8 % 16 == 15, sides[c], pltpu.roll(own[c], 127, 1)) for c in range(HELD)],
        [jnp.where(lane8 % 16 == 0, sides[c], pltpu.roll(own[c], 1, 1)) for c in range(HELD)],
    )
    flag = both(right_ref[24:25], left_ref[24:25])
    result, _, _ = advance(
        own, (along_z, along_x, (outer, inner)), flag, height_of((lane8 // 16).astype(F32)), par
    )
    for c, value in enumerate(with_densities(result, par)):
        edge_ref[2 * c : 2 * c + 2] = value[0:2]
    turned_ref[...] = edge_ref[...].T

    flow = None
    for z in range(CZ):
        start = (z + 1) * CX
        own = [first_ref[c, start : start + CX] for c in range(HELD)]
        along_z = (
            [first_ref[c, start + CX : start + 2 * CX] for c in range(HELD)],
            [first_ref[c, start - CX : start] for c in range(HELD)],
        )
        along_x = split(
            [
                beside_x(first_ref, c, start, xface_ref[c, z : z + 1], xface_ref[HELD + c, z : z + 1])
                for c in range(HELD)
            ]
        )
        rows = turned_ref[z * CX : (z + 1) * CX]
        along_y = split([beside_y(own[c], rows, 2 * c) for c in range(HELD)])
        result, last, flow = advance(own, (along_z, along_x, along_y), flags, height_of(z), par, flow)
        for c in range(3):
            phases_ref[c, z * CX : (z + 1) * CX] = result[c]
            solutes_ref[c, z * CX : (z + 1) * CX] = result[3 + c]
        phases_ref[3, z * CX : (z + 1) * CX] = last
        for c in range(KEPT):
            final_ref[c * ROWS + z * CX : c * ROWS + (z + 1) * CX] = result[c]

    for owner in range(64):
        send_ref[owner, 0:1] = jnp.full((1, 128), MARKER, F32)
    group = lane8 // 8
    for b in range(2):
        for q in range(4):
            parts = []
            for i in range(16):
                row = (2 * q + i // 8) * CX + b * 8 + i % 8
                parts.append(final_ref[pl.ds(row, 8, stride=ROWS)])
            for step in (8, 4, 2, 1):
                keep = (group & step) == 0
                swapped = list(parts)
                for i in range(16):
                    if i & step == 0:
                        one, two = parts[i], parts[i + step]
                        swapped[i] = jnp.where(keep, one, pltpu.roll(two, step * 8, 1))
                        swapped[i + step] = jnp.where(keep, pltpu.roll(one, 128 - step * 8, 1), two)
                parts = swapped
            for d in range(16):
                slot = slots_ref[b * 16 + d]
                send_ref[slot >> 1, pl.ds(2 * q + (slot & 1), KEPT, stride=8)] = parts[d][0:6]


def place(arrived_ref, moved_ref, sources):
    sub16 = sublanes_of(16)
    weight = jnp.zeros((16, 128), F32)
    for i in range(16):
        weight = jnp.where((sub16 == i) & (lanes_of(16) == 0), float(2**i), weight)
    masks = []
    for block in range(4):
        first = jnp.concatenate([arrived_ref[block * 16 + i, 0:1] for i in range(16)], axis=0)
        masks.append(jnp.sum(jnp.where(first < LIMIT, weight, 0.0)).astype(jnp.int32))
    count = jnp.int32(0)
    for source in range(64):
        sources[count] = source
        count = count + ((masks[source // 16] >> (source % 16)) & 1)
    for n in range(0, 16, 4):
        group = [sources[n + i] & 63 for i in range(4)]
        rows = slice(2 * n, 2 * n + 8)
        for q in range(4):
            span = slice(q * 128, (q + 1) * 128)
            parts = []
            for c in range(KEPT):
                at = 8 * c + 2 * q
                parts.append(jnp.concatenate([arrived_ref[s, at : at + 2] for s in group], axis=0))
            for c in range(3):
                moved_ref[c, rows, span] = parts[c]
                moved_ref[4 + c, rows, span] = parts[3 + c]
            moved_ref[3, rows, span] = 1.0 - (parts[0] + parts[1] + parts[2])


def shape_of(*dims):
    return jax.ShapeDtypeStruct(dims, F32)


PARAMS = pltpu.CompilerParams(vmem_limit_bytes=32 * 1024 * 1024)


def call(body, ins, outs, scratch=(), out_specs=None):
    return pl.pallas_call(
        body,
        in_specs=list(ins),
        out_specs=out_specs or [VMEM] * len(outs),
        out_shape=list(outs),
        scratch_shapes=list(scratch),
        compiler_params=PARAMS,
        cost_estimate=pl.CostEstimate(flops=0, bytes_accessed=1000000, transcendentals=0),
    )


def shifted(value, axis, by, wrap):
    count = lax.axis_size(axis)
    pairs = [
        (source, (source + by) % count) for source in range(count) if wrap or 0 <= source + by < count
    ]
    return lax.ppermute(value, axis, pairs)


def stepped(
    with_second, phases, solutes, melt, shift_rows, flags, balance,
    stiffness, barrier, coupling, slope, diffusivity, release,
):
    slab = lax.axis_index("gz").astype(jnp.int32).reshape(1)
    small = jnp.concatenate([flags.reshape(32), shift_rows])
    plain = jnp.concatenate([melt, barrier, slope])
    table = jnp.concatenate([stiffness, coupling, diffusivity, release], axis=1)
    bulk, second, even, odd, strip, columns, meta = call(
        pack_z,
        [VMEM] * 2 + [SMEM] * 2,
        [
            shape_of(KEPT * ROWS + CX, 128), shape_of(KEPT * 2 * CX, 128),
            shape_of(PAIRED, 128), shape_of(PAIRED, 128), shape_of(PAIRED, 128), shape_of(ROWS, 128), shape_of(24, 128),
        ],
        [pltpu.VMEM((PAIRED, 128), F32)],
    )(phases.reshape(4, ROWS, CY), solutes.reshape(3, ROWS, CY), small, slab)
    even = lax.ppermute(even, "gz", [(0, 1), (1, 0), (2, 3), (3, 2)])
    odd = lax.ppermute(odd, "gz", [(1, 2), (2, 1)])
    above2 = shifted(second, "gz", -2, False) if with_second else second
    meta, plain = lax.optimization_barrier((meta, plain))

    low, high = call(
        pack_x,
        [VMEM] * 6 + [SMEM],
        [shape_of(KEPT * X_ROWS + 4, 128)] * 2,
        [pltpu.VMEM((17 * STRIP, 128), F32)],
    )(strip, even, odd, above2, meta, plain.reshape(1, 11), slab)
    before = shifted(high, "gx", 1, True)
    after = shifted(low, "gx", -1, True)
    late_bulk, _ = lax.optimization_barrier((bulk, low))
    above = shifted(late_bulk, "gz", -1, False)
    turned, slots = call(
        turn_columns,
        [VMEM] * 6 + [SMEM] * 2,
        [shape_of(56, 128), jax.ShapeDtypeStruct((32,), jnp.int32)],
        [pltpu.VMEM((17 * CX, 128), F32), pltpu.VMEM((128, 128), F32), pltpu.SMEM((64,), jnp.int32)],
        out_specs=[VMEM, SMEM],
    )(columns, even, odd, above2, meta, plain.reshape(1, 11), slab, balance)

    face_up, face_down = call(
        pack_y, [VMEM] * 3, [shape_of(32, 128)] * 2, [pltpu.VMEM((128, 128), F32)]
    )(turned, before, after)
    left = shifted(face_up, "gy", 1, True)
    right = shifted(face_down, "gy", -1, True)

    phases_out, solutes_out, send = call(
        steps,
        [VMEM] * 11 + [SMEM] * 4,
        [shape_of(4, ROWS, CY), shape_of(3, ROWS, CY), shape_of(64, 48, 128)],
        [
            pltpu.VMEM((KEPT, 19 * CX, 128), F32),
            pltpu.VMEM((HELD, WINDOW * CX, 128), F32),
            pltpu.VMEM((128, 128), F32),
            pltpu.VMEM((128, 128), F32),
            pltpu.VMEM((HELD, 10 * CX, 128), F32),
            pltpu.VMEM((2 * HELD, 24, 128), F32),
            pltpu.VMEM((2 * HELD, 8, 128), F32),
            pltpu.VMEM((8 * ROWS, 128), F32),
        ],
    )(
        bulk, above, above2, even, odd, before, after, turned, left, right, meta, slots, slab, plain, table,
    )
    return phases_out.reshape(4, CZ, CX, CY), solutes_out.reshape(3, CZ, CX, CY), send


def per_device(phases, solutes, melt, shift_rows, *rest):
    phases_out, solutes_out, send = lax.cond(
        shift_rows[0] >= 7,
        functools.partial(stepped, True),
        functools.partial(stepped, False),
        phases, solutes, melt, shift_rows, *rest,
    )
    arrived = lax.all_to_all(send, ("gx", "gy"), split_axis=0, concat_axis=0, tiled=True)
    (moved,) = call(place, [VMEM], [shape_of(7, 32, 512)], [pltpu.SMEM((65,), jnp.int32)])(arrived)
    return phases_out, solutes_out, jnp.transpose(moved, (1, 0, 2))


def solution(mesh):
    block = P(None, "gz", "gx", "gy")
    table = P("gz", "gx", "gy", None)
    return jax.shard_map(
        per_device,
        mesh=mesh,
        in_specs=(block, block, P(), P(), table, table, P(), P(), P(), P(), P(), P()),
        out_specs=(block, block, P(("gz", "gx", "gy"), None, None)),
        check_vma=False,
    )
```
